32 devices in a mesh: own: 16 (over z, y, core), dp: 2 (over x).
Axes of the slice: x: 2, y: 2, z: 4, core: 2. Of those that a mesh axis runs over, the one named last changes fastest.
Arguments:
- tokens: bfloat16 [16, 1024, 768], P('own', 'dp'), may hold values from -6 to 6
- tie_vector: int32 [3], replicated, may hold values from 0 to 1, as said below
- qkv_weight: bfloat16 [2, 768, 2304], P(None, 'own'), may hold values from -0.21875 to 0.21875
- out_weight: bfloat16 [2, 768, 768], P(None, 'own'), may hold values from -0.875 to 0.875
- fc_weight: bfloat16 [2, 768, 3072], P(None, 'own'), may hold values from -0.21875 to 0.21875
- proj_weight: bfloat16 [2, 3072, 768], P(None, 'own'), may hold values from -0.109375 to 0.109375
- norm_gains: bfloat16 [2, 2, 768], P(None, None, 'own'), may hold values from 0.25 to 1.75
- norm_shifts: bfloat16 [2, 2, 768], P(None, None, 'own'), may hold values from -1.5 to 1.5
- bias_model: bfloat16 [2, 4, 768], P(None, None, 'own'), may hold values from -1.5 to 1.5
- bias_hidden: bfloat16 [2, 3072], P(None, 'own'), may hold values from -2.5 to 2.5
- cotangent: bfloat16 [16, 1024, 768], P('own', 'dp'), may hold values from -6 to 6
Outputs:
- output: bfloat16 [16, 1024, 768], P('own', 'dp')
- input_grad: bfloat16 [16, 1024, 768], P('own', 'dp')
- qkv_grad: float32 [2, 768, 2304], P(None, 'own')
- out_grad: float32 [2, 768, 768], P(None, 'own')
- fc_grad: float32 [2, 768, 3072], P(None, 'own')
- proj_grad: float32 [2, 3072, 768], P(None, 'own')
- gains_grad: float32 [2, 2, 768], P(None, None, 'own')
- shifts_grad: float32 [2, 2, 768], P(None, None, 'own')
- bias_model_grad: float32 [2, 4, 768], P(None, None, 'own')
- bias_hidden_grad: float32 [2, 3072], P(None, 'own')
The draws below stay inside these ranges and needn't reach their ends.
Inputs may be any that keep to these rules, and one draw needn't show every extreme that they name: `tie_vector`: each of the 2 sources is read by at least one of the 3 layers.
All inputs are finite; a program needn't handle non-finite values.
Results may differ from the reference program's by a relative error of at most 0.018.
Values may be sent and summed in bfloat16 or wider, within the bound.
No kernel may reach another device: no remote copies, remote signals or barrier semaphores. Data moves between devices by JAX's collectives and lax.ppermute only.
A program may use at most 448 MiB of HBM per device.

```python
import math
import jax
import jax.numpy as jnp
from jax import lax

D = 768
HEADS = 12
FF = 3072
LEN = 1024
SOURCES = 2
USES = 3
SEQUENCES = 16


def draw_tie_vector(key, part):
    key = jax.random.fold_in(key, 11)
    key_perm, key_more, key_mix = jax.random.split(key, 3)
    base = jax.random.permutation(key_perm, jnp.arange(SOURCES, dtype=jnp.int32))
    extra = jax.random.randint(key_more, (USES - SOURCES,), 0, SOURCES, dtype=jnp.int32)
    return jax.random.permutation(key_mix, jnp.concatenate([base, extra])).astype(jnp.int32)


def block_levels(rng, shape, pieces, low, top_value):
    gain, own = 1.0, jax.random.fold_in(rng, 6)
    for position, parts in pieces:
        heights = jnp.exp(jax.random.uniform(jax.random.fold_in(own, position), (parts,), jnp.float32, low / len(pieces), top_value / len(pieces)))
        gain = gain * jnp.repeat(heights, shape[position] // parts).reshape([-1 if axis == position else 1 for axis in range(len(shape))])
    return gain


def gaussian(rng, shape, width, reach, pieces=(), held_as=jnp.bfloat16):
    values = width * jax.random.normal(rng, shape, jnp.float32)
    if pieces:
        values = values * block_levels(rng, shape, pieces, -0.22, 0.18)
    return jnp.clip(values, -reach, reach).astype(held_as)


def setup_inputs(seed: int = 0) -> dict:
    key_of = jax.random.split(jax.random.key(seed), 12)
    tokens = gaussian(key_of[0], (SEQUENCES, LEN, D), 1.0, 6.0, ((0, 16), (1, 2)))
    tie_vector = draw_tie_vector(jax.random.fold_in(key_of[11], 71), 0)
    qkv_weight = gaussian(key_of[2], (SOURCES, D, 3 * D), D ** -0.5, 0.21875, ((1, 16),))
    out_weight = gaussian(key_of[3], (SOURCES, D, D), (D // 16) ** -0.5, 0.875, ((1, 16),))
    fc_weight = gaussian(key_of[4], (SOURCES, D, FF), D ** -0.5, 0.21875, ((1, 16),))
    proj_weight = gaussian(key_of[5], (SOURCES, FF, D), FF ** -0.5, 0.109375, ((1, 16),))
    norm_gains = jnp.clip(1.0 + 0.15 * jax.random.normal(key_of[6], (SOURCES, 2, D), jnp.float32), 0.25, 1.75).astype(jnp.bfloat16)
    norm_shifts = gaussian(key_of[7], (SOURCES, 2, D), 0.3, 1.5, ((2, 16),))
    bias_model = gaussian(key_of[8], (SOURCES, 4, D), 0.3, 1.5, ((2, 16),))
    bias_hidden = gaussian(key_of[9], (SOURCES, FF), 0.5, 2.5, ((1, 16),))
    cotangent = gaussian(key_of[10], (SEQUENCES, LEN, D), 1.0, 6.0, ((0, 16), (1, 2)))
    return dict(tokens=tokens, tie_vector=tie_vector, qkv_weight=qkv_weight, out_weight=out_weight, fc_weight=fc_weight, proj_weight=proj_weight, norm_gains=norm_gains, norm_shifts=norm_shifts, bias_model=bias_model, bias_hidden=bias_hidden, cotangent=cotangent)


HIGHEST_PREC = lax.Precision.HIGHEST
NORM_EPS = 1e-05

@jax.custom_vjp
def low(v):
    return lax.optimization_barrier(v.astype(jnp.bfloat16)).astype(jnp.float32)

@jax.custom_vjp
def low_back(v):
    return v

def low_keep(v):
    return (low(v), None)

def low_pass(kept, grad):
    return (grad,)

def back_keep(v):
    return (v, None)

def back_low(kept, grad):
    return (low(grad),)
low.defvjp(low_keep, low_pass)
low_back.defvjp(back_keep, back_low)

def norm_apply(values_in, gain_vec, shift_vec):
    centre = lax.optimization_barrier(jnp.mean(values_in, -1, keepdims=True))
    centred = values_in - centre
    spread = lax.optimization_barrier(jnp.mean(centred * centred, -1, keepdims=True))
    return centred * lax.rsqrt(spread + NORM_EPS) * gain_vec + shift_vec

def gelu_apply(pre_act):
    return 0.5 * pre_act * (1.0 + jnp.tanh(0.7978845608028654 * (pre_act + 0.044715 * pre_act * pre_act * pre_act)))

def layer_apply(resid, weights):
    qkv_w, out_w, fc_w, proj_w, gains, shifts, bias_m, bias_h = weights
    seq_count = resid.shape[0]
    head_dim = D // HEADS
    scale = float(head_dim) ** (-0.5)
    normed = low(norm_apply(resid, gains[0], shifts[0]))
    joined = jnp.dot(normed, qkv_w, precision=HIGHEST_PREC)
    queries = low(low_back(joined[..., :D] + bias_m[0]))
    keys_all = low(low_back(joined[..., D:2 * D]))
    values_all = low(low_back(joined[..., 2 * D:] + bias_m[1]))
    shape_heads = (seq_count, LEN, HEADS, head_dim)
    scores = low_back(jnp.einsum('bqhd,bkhd->bhqk', queries.reshape(shape_heads), keys_all.reshape(shape_heads), precision=HIGHEST_PREC) * scale)
    positions = jnp.arange(LEN)
    allowed = positions[None, :] <= positions[:, None]
    masked = jnp.where(allowed, scores, -1e+30)
    row_top = lax.optimization_barrier(jnp.max(masked, -1, keepdims=True))
    expo_rows = jnp.where(allowed, jnp.exp(masked - row_top), 0.0)
    attn_probs = low(expo_rows / lax.optimization_barrier(jnp.sum(expo_rows, -1, keepdims=True)))
    mixed = jnp.einsum('bhqk,bkhd->bqhd', attn_probs, values_all.reshape(shape_heads), precision=HIGHEST_PREC).reshape(seq_count, LEN, D)
    mixed = low(low_back(mixed))
    attn_out = low_back(jnp.dot(mixed, out_w, precision=HIGHEST_PREC) + bias_m[2])
    middle = resid + attn_out
    normed_mlp = low(norm_apply(middle, gains[1], shifts[1]))
    pre_act = low_back(jnp.dot(normed_mlp, fc_w, precision=HIGHEST_PREC) + bias_h)
    activated = low(gelu_apply(pre_act))
    branch = low_back(jnp.dot(activated, proj_w, precision=HIGHEST_PREC) + bias_m[3])
    return middle + branch

def block_apply(resid, params, tie_vector):
    for layer_index in range(USES):
        source = tie_vector[layer_index]
        weights = tuple((table[source] for table in params))
        resid = layer_apply(resid, weights)
    return resid

def reference(tokens, tie_vector, qkv_weight, out_weight, fc_weight, proj_weight, norm_gains, norm_shifts, bias_model, bias_hidden, cotangent):
    params = tuple((table.astype(jnp.float32) for table in (qkv_weight, out_weight, fc_weight, proj_weight, norm_gains, norm_shifts, bias_model, bias_hidden)))
    inputs = tokens.astype(jnp.float32)
    group_size = math.gcd(SEQUENCES, 4)

    def whole_block(resid_all, params_all):
        grouped = resid_all.reshape(SEQUENCES // group_size, group_size, LEN, D)

        def group_step(carry, piece):
            result = jax.checkpoint(lambda part, tables: block_apply(part, tables, tie_vector))(piece, params_all)
            return (carry, result)
        _, results = lax.scan(group_step, jnp.zeros((), jnp.float32), grouped)
        return results.reshape(SEQUENCES, LEN, D)
    result, pullback = jax.vjp(whole_block, inputs, params)
    input_grad, param_grads = pullback(cotangent.astype(jnp.float32))
    return (result.astype(jnp.bfloat16), input_grad.astype(jnp.bfloat16), param_grads[0], param_grads[1], param_grads[2], param_grads[3], param_grads[4], param_grads[5], param_grads[6], param_grads[7])
```

```python
import functools

import jax
import jax.numpy as jnp
from jax import lax
from jax.experimental import pallas as pl
from jax.experimental.pallas import tpu as pltpu
from jax.sharding import PartitionSpec as P

D = 768
HEADS = 12
PAIRS = HEADS // 2
FF = 3072
NC = FF // D
NG = 16
GR = D // NG
PR = FF // NG
SMALL = 16
NORM_EPS = 1e-05
GELU_C = 0.7978845608028654
GELU_A = 0.044715
BF = jnp.bfloat16
F32 = jnp.float32
VMEM_LIMIT = 50 * 2**20


def dot(a, b):
    return lax.dot_general(a, b, (((1,), (0,)), ((), ())), preferred_element_type=F32)


def dot_nt(a, b):
    return lax.dot_general(a, b, (((1,), (1,)), ((), ())), preferred_element_type=F32)


def dot_tn(a, b):
    return lax.dot_general(a, b, (((0,), (0,)), ((), ())), preferred_element_type=F32)


def norm_parts(x):
    centred = x - jnp.mean(x, -1, keepdims=True)
    rstd = lax.rsqrt(jnp.mean(centred * centred, -1, keepdims=True) + NORM_EPS)
    return centred * rstd, rstd


def norm_back(xhat, rstd, gain, dy):
    dxh = dy * gain
    return rstd * (
        dxh
        - jnp.mean(dxh, -1, keepdims=True)
        - xhat * jnp.mean(dxh * xhat, -1, keepdims=True)
    )


def params_of(prm):
    return jnp.sum(prm[...].astype(F32), (0, 1))


SEL, CORE, PLANE, YPOS, ZPOS, ZLOW, ZHIGH, UPS = range(8)
COUNTS = {"a": 1, "b": 1, "a2": 2, "b4": 4}
A_ROWS, B_ROWS = 4 * GR + SMALL, NC * GR + PR


class Weights:
    def __init__(self, kinds, refs, meta):
        self.meta, self.srcs = meta, []
        for kind in kinds:
            parts = []
            for part in kind:
                parts.append((part, refs[: COUNTS[part]]))
                refs = refs[COUNTS[part] :]
            self.srcs.append(parts)

    @staticmethod
    def count(kinds):
        return sum(COUNTS[part] for kind in kinds for part in kind)

    def pair(self, refs, view, dst, sem):
        core = self.meta[CORE]
        pltpu.make_async_copy(view(refs[0]), dst.at[:, core], sem).start()
        pltpu.make_async_copy(view(refs[1]), dst.at[:, 1 - core], sem).start()

    def of_half(self, refs, half, view, dst, sem):
        mine = self.meta[PLANE] == half
        pl.when(mine)(lambda: self.pair(refs[:2], view, dst, sem))
        pl.when(jnp.logical_not(mine))(lambda: self.pair(refs[2:], view, dst, sem))

    def each(self, part, copy):
        if len(self.srcs) == 1:
            copy(*self.srcs[0][part])
        else:
            for number, parts in enumerate(self.srcs):
                pl.when(self.meta[SEL] == number)(functools.partial(copy, *parts[part]))

    def start_a(self, row, size, dst, sem):
        def copy(kind, refs):
            if kind == "a":
                pltpu.make_async_copy(rows_of(refs[0], row, size), dst, sem).start()
            else:
                self.pair(refs, lambda r: rows_of(r, row, size), dst, sem)

        self.each(0, copy)

    def start_qk(self, dst, sem):
        self.start_a(0, 2 * GR, dst, sem)

    def start_v(self, dst, sem):
        self.start_a(2 * GR, GR, dst, sem)

    def start_out(self, dst, sem):
        self.start_a(3 * GR, GR, dst, sem)

    def start_small(self, dst, sem):
        self.start_a(4 * GR, SMALL, dst, sem)

    def start_in(self, c, dst, sem):
        def copy(kind, refs):
            if kind == "b":
                view = rows_of(refs[0], A_ROWS + c * GR, GR)
                pltpu.make_async_copy(view, dst, sem).start()
            else:
                half, at = divmod(c, NC // 2)
                self.of_half(refs, half, lambda r: rows_of(r, at * GR, GR), dst, sem)

        self.each(1, copy)

    def start_proj(self, c, dst, sem):
        owners = pl.ds(c * (NG // 2 // NC), NG // 2 // NC)

        def copy(kind, refs):
            if kind == "b":
                view = rows_of(refs[0].at[owners], A_ROWS + NC * GR, PR)
                pltpu.make_async_copy(view, dst, sem).start()
                return
            size = PR // 2
            view = lambda r: rows_of(r.at[owners], NC // 2 * GR, size)
            for half in range(2):
                part = dst.at[:, :, pl.ds(half * size, size), :]
                self.of_half(refs, half, view, part, sem)

        self.each(1, copy)


def rows_of(ref, row, size):
    if len(ref.shape) == 4:
        return ref.at[:, :, pl.ds(row, size), :]
    return ref.at[:, pl.ds(row, size), :]


def landed(dst, sem):
    pltpu.make_async_copy(dst, dst, sem).wait()


def qkv_kernel(kinds, meta, resid, *rest):
    nw = Weights.count(kinds)
    weights = Weights(kinds, rest[:nw], meta)
    q_out, kv_out, wqk, wv, prm, sems = rest[nw:]
    weights.start_small(prm, sems.at[0])
    weights.start_qk(wqk, sems.at[1])
    weights.start_v(wv, sems.at[2])
    xhat, _ = norm_parts(resid[...])
    landed(prm, sems.at[0])
    par = params_of(prm)
    normed = (xhat * par[0:1] + par[2:3]).astype(BF)
    landed(wqk, sems.at[1])
    kv_out[0] = dot(normed, wqk[:, :, GR:, :].reshape(D, D)).astype(BF)
    landed(wv, sems.at[2])
    kv_out[1] = (dot(normed, wv[...].reshape(D, D)) + par[5:6]).astype(BF)
    q = (dot(normed, wqk[:, :, :GR, :].reshape(D, D)) + par[4:5]).astype(BF)
    q_out[...] = q * BF((D // HEADS) ** -0.5)


def by_head(x, first):
    return jnp.concatenate([jnp.where(first, x, 0), jnp.where(first, 0, x)], 0)


def pair_masks(half, axis):
    lane = lax.broadcasted_iota(jnp.int32, (1, 2 * D // HEADS), 1)
    shape = (2 * half, half) if axis == 0 else (half, 2 * half)
    query = lax.broadcasted_iota(jnp.int32, shape, axis)
    query = jnp.where(query >= half, query - half, query)
    key = lax.broadcasted_iota(jnp.int32, shape, 1 - axis)
    return lane < D // HEADS, key <= query


def attn_fwd_kernel(others, meta, q_ref, ko, vo, kx, vx, mixed, lse, lse_scr):
    step = pl.program_id(0)
    rows = q_ref.shape[0]
    half = rows // 2
    lanes = 2 * D // HEADS
    first, tri = pair_masks(half, 0)
    highs = [meta[UPS + t] > 0 for t in range(others)]
    q_lo, q_hi = by_head(q_ref[:half], first), by_head(q_ref[half:], first)
    ones = jnp.ones((half, 128), BF)
    wide = lambda v: jnp.concatenate([v, ones], 1)
    s_ll = jnp.where(tri, dot_nt(q_lo, ko[0, :half]), -1e30)
    s_hl = dot_nt(q_hi, ko[0, :half])
    s_hh = jnp.where(tri, dot_nt(q_hi, ko[0, half:]), -1e30)
    top = jnp.maximum(s_hl, s_hh)
    s_ho, s_x, m_x = [], [], []
    for t in range(others):
        s_ho.append(dot_nt(q_hi, kx[t, 0, :half]))
        top = jnp.maximum(top, s_ho[t])
        k_x = jnp.where(highs[t], kx[t, 0, half:], kx[t, 0, :half])
        s_x.append(dot_nt(jnp.where(highs[t], q_hi, q_lo), k_x))
        m_x.append(jnp.max(s_x[t], -1, keepdims=True))
    m_lo = jnp.max(s_ll, -1, keepdims=True)
    m_hi = jnp.max(top, -1, keepdims=True)
    for t in range(others):
        m_hi = jnp.maximum(m_hi, jnp.where(highs[t], m_x[t], -1e30))
        m_lo = jnp.maximum(m_lo, jnp.where(highs[t], -1e30, m_x[t]))
    prob = lambda s, m: jnp.exp(s - m).astype(BF)
    v_lo = wide(vo[0, :half])
    o_lo = dot(prob(s_ll, m_lo), v_lo)
    o_hi = dot(prob(s_hl, m_hi), v_lo) + dot(prob(s_hh, m_hi), wide(vo[0, half:]))
    for t in range(others):
        v_x = jnp.where(highs[t], vx[t, 0, half:], vx[t, 0, :half])
        o_x = dot(prob(s_x[t], jnp.where(highs[t], m_hi, m_lo)), wide(v_x))
        o_hi = o_hi + dot(prob(s_ho[t], m_hi), wide(vx[t, 0, :half]))
        o_hi = o_hi + jnp.where(highs[t], o_x, 0.0)
        o_lo = o_lo + jnp.where(highs[t], 0.0, o_x)
    at = lax.broadcasted_iota(jnp.int32, (1, 128), 1)
    for part, (o, m) in enumerate(((o_lo, m_lo), (o_hi, m_hi))):
        out_rows = slice(part * half, (part + 1) * half)
        total = o[:, lanes:]
        norm = o[:, :lanes] / total
        mixed[out_rows] = jnp.where(first, norm[:half], norm[half:]).astype(BF)
        log = m + jnp.log(total)
        old = jnp.where(at == 2 * step, log[:half], lse_scr[out_rows])
        lse_scr[out_rows] = jnp.where(at == 2 * step + 1, log[half:], old)

    @pl.when(step == PAIRS - 1)
    def _():
        lse[0] = jnp.transpose(lse_scr[:half])[:16]
        lse[1] = jnp.transpose(lse_scr[half:])[:16]


def mlp_kernel(kinds, meta, resid, mixed, *rest):
    nw = Weights.count(kinds)
    weights = Weights(kinds, rest[:nw], meta)
    middle, pre_out, result, ow, prm, fw, pw, nm, acc, par, sems = rest[nw:]
    weights.start_out(ow, sems.at[0])
    weights.start_small(prm, sems.at[1])
    for c in range(NC):
        weights.start_in(c, fw.at[c], sems.at[2 + c])
        weights.start_proj(c, pw.at[c], sems.at[2 + NC + c])
    landed(prm, sems.at[1])
    par[...] = params_of(prm)
    landed(ow, sems.at[0])
    mid = resid[...] + dot(mixed[...], ow[...].reshape(D, D)) + par[6:7]
    middle[...] = mid
    xhat, _ = norm_parts(mid)
    nm[...] = (xhat * par[1:2] + par[3:4]).astype(BF)
    acc[...] = mid + par[7:8]

    def chunk(c, carry):
        landed(fw.at[c], sems.at[2 + c])
        pre = dot(nm[...], fw[c].reshape(D, D)) + par[pl.ds(8 + c, 1), :]
        pre_out[c] = pre.astype(BF)
        act = 0.5 * pre * (1.0 + jnp.tanh(GELU_C * (pre + GELU_A * pre * pre * pre)))
        landed(pw.at[c], sems.at[2 + NC + c])
        acc[...] += dot(act.astype(BF), pw[c].reshape(D, D))
        return carry

    lax.fori_loop(0, NC, chunk, 0)
    result[...] = acc[...]


def sort_terms(mode, keep, term, prev):
    if mode == 0:
        return (term,)
    if mode == 2:
        return (term + prev.astype(F32),)
    prev = prev.astype(F32)
    mine, old = keep
    return (mine * term + old * prev, (1.0 - mine) * term + (1.0 - old) * prev)


def to_cores(buf, mine, other, core, sem_mine, sem_other):
    return [
        pltpu.make_async_copy(buf.at[:, core], mine, sem_mine),
        pltpu.make_async_copy(buf.at[:, 1 - core], other, sem_other),
    ]


def mlp_back_kernel(kinds, mode, meta, keep_ref, dres, mid, pre, mixed, *rest):
    nw = Weights.count(kinds)
    weights = Weights(kinds, rest[:nw], meta)
    rest = rest[nw:]
    prev_b, prev_o = rest[:2] if mode else (None, None)
    rest = rest[2:] if mode else rest
    nout = 2 if mode == 1 else 1
    d_middle, d_mixed, dt, small = rest[:4]
    rest = rest[4:]
    done = mode > 0
    if done:
        done_mine, done_other, done_o = rest[:3]
        rest = rest[3:]
    if mode < 2:
        open_b, open_o = rest[:2]
        rest = rest[2:]
    (ow, prm, fw, pw, nm, acc, par, d_br, sems, osems) = rest[:10]
    stage = rest[10:]
    bufs = [stage[3 * i : 3 * i + 3] for i in range(nout)]
    core = meta[CORE]
    groups = NG // 2 // NC
    keep = (keep_ref[0], keep_ref[1])
    weights.start_small(prm, sems.at[1])
    for c in range(NC):
        weights.start_proj(c, pw.at[c], sems.at[2 + NC + c])
        weights.start_in(c, fw.at[c], sems.at[2 + c])
    weights.start_out(ow, sems.at[0])

    def in_view(ref, c):
        return rows_of(ref, c * GR, GR)

    def proj_view(ref, c):
        return rows_of(ref.at[pl.ds(c * groups, groups)], NC * GR, PR)

    def prev_copies(c):
        slot = lax.rem(c, 2)
        return [
            pltpu.make_async_copy(
                in_view(prev_b, c), bufs[-1][0].at[slot], sems.at[2 + 2 * NC + c]
            ),
            pltpu.make_async_copy(
                proj_view(prev_b, c), bufs[-1][1].at[slot], sems.at[2 + 3 * NC + c]
            ),
        ]

    if mode:
        for copy in prev_copies(0):
            copy.start()
        prev_o_copy = pltpu.make_async_copy(prev_o, bufs[-1][2], sems.at[2 + 4 * NC])
        prev_o_copy.start()
    landed(prm, sems.at[1])
    par[...] = params_of(prm)
    xhat, _ = norm_parts(mid[...])
    nm[...] = jnp.transpose((xhat * par[1:2] + par[3:4]).astype(BF))
    d_br[...] = dres[...].astype(BF)
    small[...] = jnp.zeros_like(small)
    small[7:8, :] = jnp.sum(d_br[...].astype(F32), 0, keepdims=True)
    ones = jnp.ones((8, d_br.shape[0]), BF)

    def out_copies(c):
        slot = lax.rem(c, 2)
        copies = []
        if done:
            f, j = bufs[0][0].at[slot], bufs[0][1].at[slot]
            sem = lambda k: osems.at[k, c]
            copies += to_cores(
                f, in_view(done_mine, c), in_view(done_other, c), core, sem(0), sem(1)
            )
            copies += to_cores(
                j, proj_view(done_mine, c), proj_view(done_other, c), core, sem(2), sem(3)
            )
        if mode < 2:
            f, j = bufs[-1][0].at[slot], bufs[-1][1].at[slot]
            copies.append(pltpu.make_async_copy(f, in_view(open_b, c), osems.at[4, c]))
            copies.append(pltpu.make_async_copy(j, proj_view(open_b, c), osems.at[5, c]))
        return copies

    acc[...] = jnp.zeros_like(acc)

    def chunk(c, carry):
        slot = lax.rem(c, 2)
        landed(pw.at[c], sems.at[2 + NC + c])
        d_act = dot_nt(pw[c].reshape(D, D), d_br[...])
        x = jnp.transpose(pre[c]).astype(F32)
        x2 = x * x
        th = jnp.tanh(x * (GELU_C + GELU_C * GELU_A * x2))
        up = 0.5 + 0.5 * th
        act = (x * up).astype(BF)
        slope = up + (x * (0.5 - 0.5 * th * th)) * (GELU_C + 3.0 * GELU_C * GELU_A * x2)
        d_pre = (d_act * slope).astype(BF)
        small[pl.ds(8 + c, 1), :] = dot_nt(ones, d_pre)[0:1]
        landed(fw.at[c], sems.at[2 + c])
        acc[...] += dot(fw[c].reshape(D, D), d_pre)
        g_fc = dot_nt(nm[...], d_pre)
        g_proj = dot(act, d_br[...])

        @pl.when(c > 0)
        def _():
            for copy in out_copies(c - 1):
                copy.wait()

        if mode:

            @pl.when(c < NC - 1)
            def _():
                for copy in prev_copies(c + 1):
                    copy.start()

            for copy in prev_copies(c):
                copy.wait()
        for part, val in ((0, g_fc), (1, g_proj)):
            prev = bufs[-1][part][slot].reshape(D, D) if mode else None
            for which, term in enumerate(sort_terms(mode, keep, val, prev)):
                ref = bufs[which][part]
                ref[slot] = term.astype(BF).reshape(ref.shape[1:])
        for copy in out_copies(c):
            copy.start()
        return carry

    lax.fori_loop(0, NC, chunk, 0)
    xhat, rstd = norm_parts(mid[...])
    dy = jnp.transpose(acc[...])
    small[1:2, :] = jnp.sum(dy * xhat, 0, keepdims=True)
    small[3:4, :] = jnp.sum(dy, 0, keepdims=True)
    d_mid = dres[...] + norm_back(xhat, rstd, par[1:2], dy)
    d_middle[...] = d_mid
    d_attn = d_mid.astype(BF)
    small[6:7, :] = jnp.sum(d_attn.astype(F32), 0, keepdims=True)
    landed(ow, sems.at[0])
    d_mix = dot_nt(d_attn, ow[...].reshape(D, D)).astype(BF)
    d_mixed[...] = d_mix
    g_out = dot_tn(mixed[...], d_attn)
    if mode:
        prev_o_copy.wait()
    prev = bufs[-1][2][...].reshape(D, D) if mode else None
    o_refs = ([done_o] if done else []) + ([open_o] if mode < 2 else [])
    o_copies = []
    for which, term in enumerate(sort_terms(mode, keep, g_out, prev)):
        bufs[which][2][...] = term.astype(BF).reshape(NG // 2, 2, GR, D)
        copy = pltpu.make_async_copy(bufs[which][2], o_refs[which], osems.at[6 + which, 0])
        copy.start()
        o_copies.append(copy)
    prod = d_mix.astype(F32) * mixed[...].astype(F32)
    big = prod.astype(BF)
    rest_part = (prod - big.astype(F32)).astype(BF)
    heads = lax.broadcasted_iota(jnp.int32, (16, D), 1) // (D // HEADS)
    ind = jnp.where(heads == lax.broadcasted_iota(jnp.int32, (16, D), 0), 1.0, 0.0).astype(BF)
    half = prod.shape[0] // 2
    for part in range(2):
        rows = slice(part * half, (part + 1) * half)
        dt[part] = dot_nt(ind, big[rows]) + dot_nt(ind, rest_part[rows])
    for copy in out_copies(NC - 1) + o_copies:
        copy.wait()


def attn_back_kernel(others, meta, q_ref, ko, vo, kx, vx, do_ref, lse, dt, dq, dkv, dkvx):
    step = pl.program_id(0)
    rows = q_ref.shape[0]
    half = rows // 2
    first, tri = pair_masks(half, 1)
    highs = [meta[UPS + t] > 0 for t in range(others)]
    scale = (D // HEADS) ** -0.5

    def stats(part):
        both = [
            (lse[part, pl.ds(2 * step + h, 1), :], dt[part, pl.ds(2 * step + h, 1), :])
            for h in range(2)
        ]
        return tuple(jnp.concatenate(x, 1) for x in zip(*both))

    q_lo, q_hi = by_head(q_ref[:half], first), by_head(q_ref[half:], first)
    do_lo, do_hi = by_head(do_ref[:half], first), by_head(do_ref[half:], first)
    low = (q_lo, do_lo) + stats(0)
    high = (q_hi, do_hi) + stats(1)

    def tile(queries, k, v, diag):
        q, do, row_lse, row_dt = queries
        p = jnp.exp(dot_nt(k, q) - row_lse)
        if diag:
            p = jnp.where(tri, p, 0.0)
        ds = (p * (dot_nt(v, do) - row_dt)).astype(BF)
        return dot_tn(ds, k), dot(ds, q), dot(p.astype(BF), do)

    k_lo, k_hi, v_lo, v_hi = ko[0, :half], ko[0, half:], vo[0, :half], vo[0, half:]
    dq_lo, dk_a, dv_a = tile(low, k_lo, v_lo, True)
    dq_hi, dk_b, dv_b = tile(high, k_lo, v_lo, False)
    dkv[0, :half] = (dk_a + dk_b).astype(BF)
    dkv[1, :half] = (dv_a + dv_b).astype(BF)
    dq_add, dk, dv = tile(high, k_hi, v_hi, True)
    dq_hi = dq_hi + dq_add
    dkv[0, half:] = dk.astype(BF)
    dkv[1, half:] = dv.astype(BF)
    for t in range(others):
        up = highs[t]
        dq_add, dk, dv = tile(high, kx[t, 0, :half], vx[t, 0, :half], False)
        dq_hi = dq_hi + dq_add
        both = tuple(jnp.where(up, a, b) for a, b in zip(high, low))
        k_x = jnp.where(up, kx[t, 0, half:], kx[t, 0, :half])
        v_x = jnp.where(up, vx[t, 0, half:], vx[t, 0, :half])
        dq_add, dk_x, dv_x = tile(both, k_x, v_x, False)
        dq_hi = dq_hi + jnp.where(up, dq_add, 0.0)
        dq_lo = dq_lo + jnp.where(up, 0.0, dq_add)
        dkvx[t, 0, :half] = (dk + jnp.where(up, 0.0, dk_x)).astype(BF)
        dkvx[t, 1, :half] = (dv + jnp.where(up, 0.0, dv_x)).astype(BF)
        dkvx[t, 0, half:] = jnp.where(up, dk_x, 0.0).astype(BF)
        dkvx[t, 1, half:] = jnp.where(up, dv_x, 0.0).astype(BF)
    dq[:half] = (jnp.where(first, dq_lo[:half], dq_lo[half:]) * scale).astype(BF)
    dq[half:] = (jnp.where(first, dq_hi[:half], dq_hi[half:]) * scale).astype(BF)


def qkv_back_kernel(
    kinds, mode, others, meta, keep_ref, resid, dq, dkv, dkvx, d_middle, small_in, *rest
):
    nw = Weights.count(kinds)
    weights = Weights(kinds, rest[:nw], meta)
    rest = rest[nw:]
    done = mode > 0
    if done:
        prev_ref, done_o = rest[:2]
        rest = rest[2:]
    nout = 2 if mode == 1 else 1
    dres = rest[0]
    rest = rest[1:]
    if done:
        done_mine, done_other = rest[:2]
        rest = rest[2:]
    if mode < 2:
        open_a = rest[0]
        rest = rest[1:]
    wqk, wv, prm, sems, osems = rest[:5]
    bufs = rest[5:]
    core = meta[CORE]
    keep = (keep_ref[0], keep_ref[1])
    weights.start_small(prm, sems.at[0])
    weights.start_qk(wqk, sems.at[1])
    weights.start_v(wv, sems.at[2])
    copies = []
    if done:
        prev_copy = pltpu.make_async_copy(prev_ref, bufs[-1], sems.at[3])
        prev_copy.start()
        copies += to_cores(
            done_o,
            rows_of(done_mine, 3 * GR, GR),
            rows_of(done_other, 3 * GR, GR),
            core,
            osems.at[0],
            osems.at[1],
        )
        for copy in copies:
            copy.start()
    landed(prm, sems.at[0])
    par = params_of(prm)
    xhat, rstd = norm_parts(resid[...])
    normed = jnp.transpose((xhat * par[0:1] + par[2:3]).astype(BF))
    parts = [dq[...]]
    for i in range(2):
        total = dkv[i].astype(F32)
        for t in range(others):
            total = total + dkvx[t, i].astype(F32)
        parts.append(total.astype(BF))
    landed(wqk, sems.at[1])
    landed(wv, sems.at[2])
    if done:
        prev_copy.wait()
    ws = [wqk[:, :, :GR, :], wqk[:, :, GR:, :], wv[...]]
    dy = 0.0
    for i, part in enumerate(parts):
        rows = slice(i * GR, (i + 1) * GR)
        dy = dy + dot_nt(part, ws[i].reshape(D, D))
        prev = bufs[-1][:, :, rows, :].reshape(D, D) if mode else None
        for which, val in enumerate(sort_terms(mode, keep, dot(normed, part), prev)):
            bufs[which][:, :, rows, :] = val.astype(BF).reshape(NG // 2, 2, GR, D)
    small = jnp.concatenate(
        [
            jnp.sum(dy * xhat, 0, keepdims=True),
            small_in[1:2],
            jnp.sum(dy, 0, keepdims=True),
            small_in[3:4],
            jnp.sum(parts[0].astype(F32), 0, keepdims=True),
            jnp.sum(parts[2].astype(F32), 0, keepdims=True),
            small_in[6:],
        ],
        0,
    )
    prev = bufs[-1][0, 0, 3 * GR :, :] if mode else None
    for which, val in enumerate(sort_terms(mode, keep, small, prev)):
        bufs[which][:, :, 3 * GR :, :] = jnp.broadcast_to(
            val.astype(BF)[None, None], (NG // 2, 2, SMALL, D)
        )
    later = []
    if done:
        for k, (lo, size, to) in enumerate(((0, 3 * GR, 0), (3 * GR, SMALL, 4 * GR))):
            later += to_cores(
                rows_of(bufs[0], lo, size),
                rows_of(done_mine, to, size),
                rows_of(done_other, to, size),
                core,
                osems.at[2 + 2 * k],
                osems.at[3 + 2 * k],
            )
    if mode < 2:
        later.append(pltpu.make_async_copy(bufs[-1], open_a, osems.at[6]))
    for copy in later:
        copy.start()
    dres[...] = d_middle[...] + norm_back(xhat, rstd, par[0:1], dy)
    for copy in copies + later:
        copy.wait()


def pack_kernel(meta, small_in, qkv, out, fc, proj, *rest):
    outs, smalls, sems = rest[:4], rest[4], rest[5]
    first, plane, at = meta[0], meta[1], meta[2]
    copies = []

    def cols(ref, src, i):
        return ref.at[src, :, pl.ds(i * D, D)]

    def copy(src, dst):
        copies.append(pltpu.make_async_copy(src, dst, sems.at[len(copies)]))
        copies[-1].start()

    for i, src in enumerate((first, 1 - first)):
        attn, ffn = outs[2 * i : 2 * i + 2]
        for k in range(NC // 2):
            col = pl.multiple_of((plane * (NC // 2) + k) * D, D)
            copy(fc.at[src, :, pl.ds(col, D)], ffn.at[pl.ds(k * GR, GR)])
        row = pl.multiple_of(plane * (PR // 2), 16)
        copy(proj.at[src, pl.ds(row, PR // 2)], ffn.at[pl.ds(NC // 2 * GR, PR // 2)])
        for k in range(3):
            copy(cols(qkv, src, k), attn.at[pl.ds(k * GR, GR)])
        copy(out.at[src], attn.at[pl.ds(3 * GR, GR)])

    lane = lax.broadcasted_iota(jnp.int32, (GR, D), 1)
    row = lax.broadcasted_iota(jnp.int32, (GR, D), 0)
    spread = jnp.where(lane == row + at * GR, 1.0, 0.0).astype(BF)
    lane = lax.broadcasted_iota(jnp.int32, (PR, D), 1)
    row = lax.broadcasted_iota(jnp.int32, (PR, D), 0)
    spread_h = jnp.where(lane == row + lax.rem(at, NG // NC) * PR, 1.0, 0.0).astype(BF)
    line = lax.broadcasted_iota(jnp.int32, (8, D), 0)
    for i, src in enumerate((first, 1 - first)):
        smalls[i, 0:8, :] = dot(small_in[src, :, :GR], spread).astype(BF)
        hid = dot(small_in[src, :, GR : GR + PR], spread_h)
        smalls[i, 8:16, :] = jnp.where(line == at // (NG // NC), hid[0:1], 0.0).astype(BF)
        copy(smalls.at[i], outs[2 * i].at[pl.ds(4 * GR, SMALL)])
    for one in copies:
        one.wait()


def assemble_kernel(meta, mine, other, whole, sems):
    copies = []
    for side, ref in enumerate((mine, other)):
        for low in range(2):
            for high in range(2):
                z = jnp.bitwise_xor(meta[ZPOS], low + 2 * high)
                y = meta[YPOS] if side == 0 else 1 - meta[YPOS]
                copies.append(
                    pltpu.make_async_copy(
                        ref.at[low, high], whole.at[z * 2 + y], sems.at[len(copies)]
                    )
                )
                copies[-1].start()
    for copy in copies:
        copy.wait()


def add_cores_kernel(segments, meta, mine, got, *outs):
    total = (mine[...].astype(F32) + got[...].astype(F32)).astype(BF)
    for i, (order, low, high, size) in enumerate(segments):
        if order == "x":
            sides, which = (total[:, low : low + size], total[:, high : high + size]), PLANE
        else:
            sides, which = (total[0:1, low : low + size], total[1:2, low : low + size]), YPOS
        outs[2 * i][...] = jnp.where(meta[which] == 0, sides[0], sides[1])
        outs[2 * i + 1][...] = jnp.where(meta[which] == 0, sides[1], sides[0])


def add_split_kernel(bits, meta, *refs):
    ins, outs = refs[: 2 * len(bits)], list(refs[2 * len(bits) :])
    for i, bit in enumerate(bits):
        mine, got = ins[2 * i], ins[2 * i + 1]
        if bit is None:
            outs.pop(0)[...] = (mine[0].astype(F32) + got[0].astype(F32)).astype(BF)
            continue
        keep, send = outs.pop(0), outs.pop(0)

        def pair(g, carry):
            for out, at in ((keep, 2 * g + meta[bit]), (send, 2 * g + 1 - meta[bit])):
                out[g] = (mine[at].astype(F32) + got[at].astype(F32)).astype(BF)
            return carry

        lax.fori_loop(0, mine.shape[0] // 2, pair, 0)


def finish_kernel(meta, *refs):
    ins, outs = refs[:12], refs[12:]
    qkv_g, out_g, fc_g, proj_g, gains_g, shifts_g, bias_g, hidden_g = outs
    first, plane, at = meta[0], meta[1], meta[2]
    low = lambda mine, peer: jnp.where(plane == 0, mine[...], peer[...])
    high = lambda mine, peer: jnp.where(plane == 0, peer[...], mine[...])
    pick = lax.broadcasted_iota(jnp.int32, (D, GR), 0) == (
        lax.broadcasted_iota(jnp.int32, (D, GR), 1) + at * GR
    )
    pick = jnp.where(pick, 1.0, 0.0).astype(BF)
    pick_h = lax.broadcasted_iota(jnp.int32, (D, PR), 0) == (
        lax.broadcasted_iota(jnp.int32, (D, PR), 1) + lax.rem(at, NG // NC) * PR
    )
    pick_h = jnp.where(pick_h, 1.0, 0.0).astype(BF)
    line = lax.broadcasted_iota(jnp.int32, (SMALL, D), 0)
    here = line == 8 + at // (NG // NC)

    def write(src, in_pair, proj_pair, qk, vo, small):
        ins_ = (low(*in_pair), high(*in_pair))
        for k in range(NC):
            rows = slice(k % (NC // 2) * GR, (k % (NC // 2) + 1) * GR)
            fc_g[src, :, k * D : (k + 1) * D] = ins_[k // (NC // 2)][rows].astype(F32)
        proj_g[src] = proj_pair[0][...].astype(F32) + proj_pair[1][...].astype(F32)
        for k, part in enumerate(qk + vo[:1]):
            qkv_g[src, :, k * D : (k + 1) * D] = part
        out_g[src] = vo[1]
        vals = dot(small, pick)
        row = jnp.sum(jnp.where(here, small.astype(F32), 0.0), 0, keepdims=True)
        hid = dot(jnp.broadcast_to(row, (8, D)).astype(BF), pick_h)
        gains_g[src] = vals[0:2]
        shifts_g[src] = vals[2:4]
        bias_g[src] = vals[4:8]
        hidden_g[src] = hid[0:1]

    for k, src in enumerate((1 - first, first)):
        ins_ = ins[4 * k : 4 * k + 4] + ins[8 + 2 * k : 10 + 2 * k]
        part_l, part_h = low(*ins_[4:6]), high(*ins_[4:6])
        write(
            src,
            ins_[0:2],
            ins_[2:4],
            (part_l[:GR].astype(F32), part_l[GR : 2 * GR].astype(F32)),
            (part_h[:GR].astype(F32), part_h[GR : 2 * GR].astype(F32)),
            part_h[2 * GR :],
        )


VM = pl.BlockSpec(memory_space=pltpu.VMEM)
SM = pl.BlockSpec(memory_space=pltpu.SMEM)
HB = pl.BlockSpec(memory_space=pl.ANY)
DMA = pltpu.SemaphoreType.DMA


def call(kernel, outs, in_specs, out_specs, scratch, flops, name, weight=8, **more):
    cost = pl.CostEstimate(flops=int(flops * weight), bytes_accessed=1024, transcendentals=0)
    return pl.pallas_call(
        kernel,
        out_shape=outs,
        in_specs=in_specs,
        out_specs=out_specs,
        scratch_shapes=scratch,
        compiler_params=pltpu.CompilerParams(vmem_limit_bytes=VMEM_LIMIT),
        cost_estimate=cost,
        name=name,
        **more,
    )


def sds(shape, dtype):
    return jax.ShapeDtypeStruct(shape, dtype)


def run_qkv(meta, resid, kinds, weights):
    rows = resid.shape[0]
    return call(
        functools.partial(qkv_kernel, kinds),
        (sds((rows, D), BF), sds((2, rows, D), BF)),
        [SM, VM] + [HB] * len(weights),
        (VM, VM),
        qkv_scratch() + [DMA((3,))],
        2 * rows * D * 3 * D,
        "qkv",
        8 if len(kinds) > 1 else 0.01,
    )(meta, resid, *weights)


def qkv_scratch():
    return [
        pltpu.VMEM((NG // 2, 2, 2 * GR, D), BF),
        pltpu.VMEM((NG // 2, 2, GR, D), BF),
        pltpu.VMEM((NG // 2, 2, SMALL, D), BF),
    ]


def pair_specs(rows, others):
    lanes = 2 * D // HEADS
    return [
        SM,
        pl.BlockSpec((rows, lanes), lambda i: (0, i)),
        pl.BlockSpec((1, rows, lanes), lambda i: (0, 0, i)),
        pl.BlockSpec((1, rows, lanes), lambda i: (1, 0, i)),
        pl.BlockSpec((others, 1, rows, lanes), lambda i: (0, 0, 0, i)),
        pl.BlockSpec((others, 1, rows, lanes), lambda i: (0, 1, 0, i)),
    ]


def run_attn(meta, q, kv, kvx, weight):
    rows, others = q.shape[0], kvx.shape[0]
    half = rows // 2
    return call(
        functools.partial(attn_fwd_kernel, others),
        (sds((rows, D), BF), sds((2, 16, half), F32)),
        pair_specs(rows, others),
        (
            pl.BlockSpec((rows, 2 * D // HEADS), lambda i: (0, i)),
            pl.BlockSpec((2, 16, half), lambda i: (0, 0, 0)),
        ),
        [pltpu.VMEM((rows, 128), F32)],
        HEADS * (3 + 2 * others) * half * half * 256 * 4,
        "attn",
        weight,
        grid=(PAIRS,),
    )(meta, q, kv, kv, kvx, kvx)


def weight_scratch(rows, flipped=False):
    shape = (D, rows) if flipped else (rows, D)
    return [
        pltpu.VMEM((NG // 2, 2, GR, D), BF),
        pltpu.VMEM((NG // 2, 2, SMALL, D), BF),
        pltpu.VMEM((NC, NG // 2, 2, GR, D), BF),
        pltpu.VMEM((NC, NG // 2 // NC, 2, PR, D), BF),
        pltpu.VMEM(shape, BF),
        pltpu.VMEM(shape, F32),
        pltpu.VMEM((SMALL, D), F32),
    ]


def run_mlp(meta, resid, mixed, kinds, weights):
    rows = resid.shape[0]
    return call(
        functools.partial(mlp_kernel, kinds),
        (sds((rows, D), F32), sds((NC, rows, D), BF), sds((rows, D), F32)),
        [SM, VM, VM] + [HB] * len(weights),
        (VM, VM, VM),
        weight_scratch(rows) + [DMA((2 + 2 * NC,))],
        2 * rows * D * (D + 2 * FF),
        "mlp",
        8 if len(kinds) > 1 else 0.01,
    )(meta, resid, mixed, *weights)


def run_mlp_back(mode, meta, keep, dres, mid, pre, mixed, kinds, weights, prev):
    rows = dres.shape[0]
    nout = 2 if mode == 1 else 1
    b_rows = NC * GR + PR
    o_shape = sds((NG // 2, 2, GR, D), BF)
    outs = ()
    if mode:
        outs += (sds((NG // 2, b_rows, D), BF),) * 2 + (o_shape,)
    if mode < 2:
        outs += (sds((NG // 2, 2, b_rows, D), BF), o_shape)
    stage = [
        pltpu.VMEM((2, NG // 2, 2, GR, D), BF),
        pltpu.VMEM((2, NG // 2 // NC, 2, PR, D), BF),
        pltpu.VMEM((NG // 2, 2, GR, D), BF),
    ] * nout
    return call(
        functools.partial(mlp_back_kernel, kinds, mode),
        (
            sds((rows, D), F32),
            sds((rows, D), BF),
            sds((2, 16, rows // 2), F32),
            sds((SMALL, D), F32),
        )
        + outs,
        [SM, SM, VM, VM, VM, VM] + [HB] * (len(weights) + len(prev)),
        (VM, VM, VM, VM) + (HB,) * len(outs),
        weight_scratch(rows, True)
        + [pltpu.VMEM((rows, D), BF), DMA((3 + 4 * NC,)), DMA((8, NC))]
        + stage,
        4 * rows * D * (D + 2 * FF),
        "mlp_back",
    )(meta, keep, dres, mid, pre, mixed, *weights, *prev)


def run_attn_back(meta, q, kv, kvx, d_mixed, lse, dt):
    rows, others = q.shape[0], kvx.shape[0]
    half = rows // 2
    lanes = 2 * D // HEADS
    stat = pl.BlockSpec((2, 16, half), lambda i: (0, 0, 0))
    block = pl.BlockSpec((rows, lanes), lambda i: (0, i))
    return call(
        functools.partial(attn_back_kernel, others),
        (sds((rows, D), BF), sds((2, rows, D), BF), sds((others, 2, rows, D), BF)),
        pair_specs(rows, others) + [block, stat, stat],
        (
            block,
            pl.BlockSpec((2, rows, lanes), lambda i: (0, 0, i)),
            pl.BlockSpec((others, 2, rows, lanes), lambda i: (0, 0, 0, i)),
        ),
        [],
        HEADS * (3 + 2 * others) * half * half * 256 * 10,
        "attn_back",
        grid=(PAIRS,),
    )(meta, q, kv, kv, kvx, kvx, d_mixed, lse, dt)


def run_qkv_back(
    mode, meta, keep, resid, dq, dkv, dkvx, d_middle, small, kinds, weights, prev
):
    rows, others = resid.shape[0], dkvx.shape[0]
    nout = 2 if mode == 1 else 1
    shape = (NG // 2, 2, 3 * GR + SMALL, D)
    outs = ()
    if mode:
        outs += (sds((NG // 2, 4 * GR + SMALL, D), BF),) * 2
    if mode < 2:
        outs += (sds(shape, BF),)
    return call(
        functools.partial(qkv_back_kernel, kinds, mode, others),
        (sds((rows, D), F32),) + outs,
        [SM, SM] + [VM] * 6 + [HB] * (len(weights) + min(mode, 1)) + [VM] * min(mode, 1),
        (VM,) + (HB,) * len(outs),
        qkv_scratch() + [DMA((4,)), DMA((7,))] + [pltpu.VMEM(shape, BF)] * nout,
        4 * rows * D * 3 * D,
        "qkv_back",
    )(meta, keep, resid, dq, dkv, dkvx, d_middle, small, *weights, *prev)


def run_pack(meta, small, qkv, out, fc, proj):
    rows = (A_ROWS, B_ROWS // 2) * 2
    return call(
        pack_kernel,
        tuple(sds((r, D), BF) for r in rows),
        [SM, VM] + [HB] * 4,
        (HB,) * 4,
        [pltpu.VMEM((2, SMALL, D), BF), DMA((2 * (NC // 2 + 6),))],
        2 * 16 * PR * D,
        "pack",
    )(meta, small, qkv, out, fc, proj)


def run_assemble(meta, mine, other):
    rows = mine.shape[-2]
    return call(
        assemble_kernel,
        sds((NG // 2, rows, D), BF),
        [SM, HB, HB],
        VM,
        [DMA((NG // 2,))],
        NG * rows * D,
        "assemble",
    )(meta, mine, other)


def run_add_cores(meta, mine, got, segments, weight):
    groups, rows = mine.shape[:2]
    outs, specs = [], []
    for order, _, _, size in segments:
        step = 2 if order == "x" else 1
        outs += [sds((groups // 2 * step, size, D), BF)] * 2
        specs += [pl.BlockSpec((step, size, D), lambda i: (i, 0, 0))] * 2
    block = pl.BlockSpec((2, rows, D), lambda i: (i, 0, 0))
    return call(
        functools.partial(add_cores_kernel, segments),
        outs,
        [SM, block, block],
        specs,
        [],
        mine.size * weight,
        "add_cores",
        grid=(groups // 2,),
    )(meta, mine, got)


def run_add_split(meta, bits, pairs, weight):
    outs = []
    for bit, (mine, _) in zip(bits, pairs):
        groups, rows = mine.shape[:2]
        if bit is None:
            outs.append(sds((rows, D), BF))
        else:
            outs += [sds((groups // 2, rows, D), BF)] * 2
    ins = [x for pair in pairs for x in pair]
    return call(
        functools.partial(add_split_kernel, bits),
        outs,
        [SM] + [VM] * len(ins),
        [VM] * len(outs),
        [],
        sum(x.size for x in ins) * weight,
        "add_split",
    )(meta, *ins)


def run_finish(meta, parts):
    outs = (
        sds((2, GR, 3 * D), F32),
        sds((2, GR, D), F32),
        sds((2, GR, FF), F32),
        sds((2, PR, D), F32),
        sds((2, 2, GR), F32),
        sds((2, 2, GR), F32),
        sds((2, 4, GR), F32),
        sds((2, 1, PR), F32),
    )
    return call(
        finish_kernel, outs, [SM] + [VM] * len(parts), (VM,) * 8, [], 2**20, "finish"
    )(meta, *parts)


def regroup(packed, own_from, own_to, widths):
    if own_from == own_to:
        return packed
    parts, at = [], 0
    for width in widths:
        rows = width // own_from
        part = packed[:, at : at + rows].reshape(width, D)
        parts.append(part.reshape(own_to, width // own_to, D))
        at += rows
    return jnp.concatenate(parts, 1)


def blocks(table):
    return jnp.concatenate([table[:, i : i + D] for i in range(0, table.shape[1], D)], 0)


def unblock(rows, count):
    size = rows.shape[0] // count
    return jnp.concatenate([rows[i * size : (i + 1) * size] for i in range(count)], 1)


def place_small(gains, shifts, bias_m, bias_h, at):
    vecs = jnp.concatenate([gains, shifts, bias_m], 0)
    wide = lax.dynamic_update_slice(jnp.zeros((8, D), BF), vecs, (0, at * vecs.shape[1]))
    hid = lax.dynamic_update_slice(jnp.zeros((FF,), BF), bias_h, (at * bias_h.shape[0],))
    return jnp.concatenate([wide, hid.reshape(NC, D), jnp.zeros((SMALL - 8 - NC, D), BF)], 0)


def per_device(own, n, tokens, tie, qkv_w, out_w, fc_w, proj_w, gains, shifts, bias_m, bias_h, cotangent):
    axes = ("own", "dp")
    o = lax.axis_index("own")
    d = lax.axis_index("dp")
    core = o % 2
    rows = tokens.shape[1]
    half = rows // 2
    others = n - 1

    def at(pair, s, j):
        return (2 * pair + j % 2) * n + s * (n // 2) + j // 2

    j = (d % (n // 2)) * 2 + core

    def place(block):
        return block if block < n else 2 * n - 1 - block

    def moves(odd):
        return [
            ((2 * pair + s) * n + dd, at(pair, s, place(2 * dd + odd)))
            for pair in range(own // 2)
            for s in range(2)
            for dd in range(n)
        ]

    def to_chip(x):
        x = x.reshape(rows, D)
        even = lax.ppermute(x[:half], axes, moves(0))
        odd = lax.ppermute(x[half:], axes, moves(1))
        return jnp.concatenate(
            [jnp.where(core == 0, even, odd), jnp.where(core == 0, odd, even)], 0
        )

    def from_chip(x):
        back = [[(b, a) for a, b in moves(odd)] for odd in range(2)]
        even = lax.ppermute(jnp.where(core == 0, x[:half], x[half:]), axes, back[0])
        odd = lax.ppermute(jnp.where(core == 0, x[half:], x[:half]), axes, back[1])
        return jnp.concatenate([even, odd], 0).reshape(tokens.shape)

    def shift(x, step):
        pairs = [
            (at(pair, s, (place_ + step) % n), at(pair, s, place_))
            for pair in range(own // 2)
            for s in range(2)
            for place_ in range(n)
        ]
        return lax.ppermute(x, axes, pairs)

    plane, y, z = d % 2, (o // 2) % 2, o // 4
    nz = own // 4

    def device(zz, yy, cc, dd):
        return ((zz * 2 + yy) * 2 + cc) * n + dd

    everyone = [
        (zz, yy, cc, dd)
        for zz in range(nz)
        for yy in range(2)
        for cc in range(2)
        for dd in range(n)
    ]

    def swap(x, axis):
        turn = {
            "core": lambda zz, yy, cc, dd: device(zz, yy, 1 - cc, dd),
            "y": lambda zz, yy, cc, dd: device(zz, 1 - yy, cc, dd),
            "x": lambda zz, yy, cc, dd: device(zz, yy, cc, dd ^ 1),
            "z1": lambda zz, yy, cc, dd: device(zz ^ 1, yy, cc, dd),
            "z2": lambda zz, yy, cc, dd: device(zz ^ 2, yy, cc, dd),
        }[axis]
        return lax.ppermute(x, axes, [(device(*at_), turn(*at_)) for at_ in everyone])

    def from_z(x, step):
        pairs = [
            (device((zz + step) % nz, yy, cc, dd), device(zz, yy, cc, dd))
            for zz, yy, cc, dd in everyone
        ]
        return lax.ppermute(x, axes, pairs)

    def after(x, *deps):
        return lax.optimization_barrier((x, *deps))[0]

    def after_all(xs, *deps):
        return lax.optimization_barrier((tuple(xs), *deps))[0]

    open_src = tie[0]
    isin = lambda u: (tie[u] != open_src).astype(jnp.int32)
    ups = [((j + t) % n > j).astype(jnp.int32) for t in range(1, n)]
    metas = [jnp.stack([isin(u), core, plane, y, z, z % 2, z // 2] + ups).astype(jnp.int32) for u in range(3)]
    keep = jnp.stack([isin(1), isin(2)]).astype(F32)
    direct = own == NG and n == 2

    if direct:
        small = jnp.concatenate([gains, shifts, bias_m], 1)
        hid = jnp.broadcast_to(bias_h[:, None], (2, 8, bias_h.shape[1]))
        packed = run_pack(
            jnp.stack([open_src, plane, o]).astype(jnp.int32),
            jnp.concatenate([small, hid], 2),
            qkv_w,
            out_w,
            fc_w,
            proj_w,
        )

        def square(x, axis):
            return jnp.stack([x, swap(x, axis)], 0)

        def cores_of(part):
            return [part, swap(part, "core")]

        twos, lines, sides = [], [], []
        for part in (packed[1], packed[3], packed[0], packed[2]):
            twos.append(square(after(part, twos[-1]) if twos else part, "z2"))
            two = after(twos[-1], lines[-1]) if lines else twos[-1]
            lines.append(square(two, "z1"))
            line = after(lines[-1], sides[-1][1]) if sides else lines[-1]
            sides.append((line, swap(line, "y")))
        resid = to_chip(after(tokens, twos[0])).astype(F32)
        dres = to_chip(after(cotangent, twos[0])).astype(F32)
        ffn = [run_assemble(after(metas[0], resid, dres, lines[1]), *sides[0])]
        peers = [swap(ffn[0], "x")]
        ffn.append(run_assemble(after(metas[0], lines[2]), *sides[1]))
        peers.append(swap(after(ffn[1], peers[0]), "x"))
        attn = run_assemble(after(metas[0], lines[3]), *sides[2])
        first_a, first_b = cores_of(attn), cores_of(ffn[0]) + cores_of(peers[0])
        kinds = (("a2", "b4"),) * 2
        second_b = cores_of(ffn[1]) + cores_of(peers[1])
        metas[0] = after(metas[0], *first_a, *first_b, *second_b[:2])
    else:
        resid = to_chip(tokens).astype(F32)
        dres = to_chip(cotangent).astype(F32)
        sources = []
        for src in (open_src, 1 - open_src):
            pick = lambda table: lax.dynamic_index_in_dim(table, src, 0, keepdims=False)
            part = jnp.concatenate(
                [blocks(pick(qkv_w)), pick(out_w), blocks(pick(fc_w)), pick(proj_w)], 0
            )
            full = lax.all_gather(part, "own", axis=0, tiled=False)
            full = regroup(full, own, NG, [D] * (4 + NC) + [FF])
            small = place_small(pick(gains), pick(shifts), pick(bias_m), pick(bias_h), o)
            small = lax.psum(small.astype(F32), "own").astype(BF)
            small = jnp.concatenate([small[None], jnp.zeros((NG - 1, SMALL, D), BF)], 0)
            full = jnp.concatenate([full[:, : 4 * GR], small, full[:, 4 * GR :]], 1)
            sources.append([full.reshape(NG // 2, 2, -1, D)])
        first_a = first_b = sources[0]
        second_a = second_b = sources[1]
        kinds = (("a", "b"),) * 2

    def weights_of(u, attn_only=False):
        many = 1 if u == 0 else 2
        arrays = first_a + ([] if attn_only else first_b)
        if u:
            arrays = arrays + second_a + ([] if attn_only else second_b)
        return tuple(kind[: 1 if attn_only else 2] for kind in kinds[:many]), arrays

    saved = []
    for u in range(3):
        meta = metas[u]
        q, kv = run_qkv(meta, resid, *weights_of(u, True))
        kvx = jnp.stack([shift(kv, t) for t in range(1, n)], 0)
        mixed, lse = run_attn(meta, q, kv, kvx, 8 if u else 0.01)
        middle, pre, result = run_mlp(meta, resid, mixed, *weights_of(u))
        if u == 0 and direct:
            second_a = cores_of(run_assemble(after(metas[1], middle, peers[1]), *sides[3]))
            metas[1] = after(metas[1], *second_a)
        saved.append((resid, q, kv, kvx, mixed, lse, middle, pre))
        resid = result
    output = from_chip(resid.astype(BF))

    def scatter_full(mine, other, widths, small_rows):
        pair = jnp.where(core == 0, jnp.stack([mine, other], 1), jnp.stack([other, mine], 1))
        grad = pair.reshape(NG, -1, D)
        body = grad.shape[1] - small_rows
        tail = grad[:1, body:]
        grad = regroup(grad[:, :body], NG, own, widths)
        if small_rows:
            tail = jnp.broadcast_to(tail, (own, small_rows, D))
            grad = jnp.concatenate([grad, tail], 1)
        part = lax.psum_scatter(grad, "own", scatter_dimension=0, tiled=False)
        return lax.psum(part, "dp").astype(F32)


    class Scatter:
        NEXT = {"x": ("y", YPOS), "y": ("z1", ZLOW), "z1": ("z2", ZHIGH), "z2": ("x", None)}

        def __init__(self, order, keep_, send):
            self.stage, self.keep, self.done = order, keep_, None
            self.got = swap(send, order)

    def step(meta, chunks, weight=1):
        moves_ = [Scatter.NEXT[one.stage] for one in chunks]
        outs = run_add_split(
            meta,
            tuple(bit for _, bit in moves_),
            [(one.keep, one.got) for one in chunks],
            weight,
        )
        first_out, outs = outs[0], list(outs)
        for one, (stage, bit) in zip(chunks, moves_):
            one.stage = stage
            one.keep = outs.pop(0)
            one.got = swap(one.keep if bit is None else outs.pop(0), stage)
            if bit is None:
                one.done = [one.keep, one.got]
        return first_out

    def scatter_start(meta, mine, got, segs, weight):
        outs = run_add_cores(meta, mine, got, segs, weight)
        return [Scatter(seg[0], *outs[2 * i : 2 * i + 2]) for i, seg in enumerate(segs)], outs[0]

    in_rows, a_rows = NC // 2 * GR, 4 * GR + SMALL
    b_segs = (("x", 0, in_rows, in_rows), ("y", NC * GR, 0, PR))
    a_segs = (("x", 0, 2 * GR, 2 * GR + SMALL),)

    prev_b, prev_a = [], []
    shares, fin, opn = {}, [], []
    wr, pr = D // own, FF // own
    for u in (2, 1, 0):
        mode = 2 - u
        meta = metas[u]
        resid, q, kv, kvx, mixed, lse, middle, pre = saved[u]
        outs = run_mlp_back(
            mode, meta, keep, dres, middle, pre, mixed, *weights_of(u), prev_b
        )
        d_middle, d_mixed, dt, small = outs[:4]
        if mode:
            mine_b, other_b, done_o = outs[4:7]
            if direct:
                got_b = swap(other_b, "core")
        prev_b = list(outs[-2:])
        if mode == 0:
            meta = after(meta, output)
        if mode == 2 and direct:
            slot = after(meta, d_mixed)
            more, last = scatter_start(slot, *fin_a, a_segs, 1)
            last = step(after(slot, last), fin, 4096)
            fin += more
            opn, last = scatter_start(after(slot, last), mine_b, got_b, b_segs, 1)
            meta = after(meta, last)
        dq, dkv, dkvx = run_attn_back(meta, q, kv, kvx, d_mixed, lse, dt)
        back = jnp.stack([shift(dkvx[t - 1], n - t) for t in range(1, n)], 0)
        if mode and direct:
            slot = after(meta, dq)
            if mode == 1:
                fin, last = scatter_start(slot, mine_b, got_b, b_segs, 4096)
            else:
                last = step(slot, fin, 4096)
            meta = after(meta, last)
        outs = run_qkv_back(
            mode,
            meta,
            keep,
            resid,
            dq,
            dkv,
            back,
            d_middle,
            small,
            *weights_of(u, True),
            prev_a + ([done_o] if mode else []),
        )
        dres = outs[0]
        prev_a = [outs[-1]]
        if not mode:
            continue
        mine_a, other_a = outs[1:3]
        if direct:
            if mode == 1:
                fin_a = (mine_a, swap(other_a, "core"))
            else:
                slot = after(metas[0], dres)
                got_a = swap(other_a, "core")
                last = step(slot, fin, 4096)
                more, last = scatter_start(after(slot, last), mine_a, got_a, a_segs, 1)
                last = step(after(slot, last), opn, 4096)
                left = [one for one in fin if one.done is None]
                last = step(after(slot, last), left, 1024)
                chunks = fin[:2] + opn + fin[2:] + more
                while any(one.done is None for one in chunks):
                    for group, weight in ((more, 1), (fin + opn, 4096)):
                        left = [one for one in group if one.done is None]
                        if left:
                            last = step(after(slot, last), left, weight)
                done = [x for one in chunks for x in one.done]
        else:
            g_b = scatter_full(mine_b, other_b, [D] * NC + [FF], 0)
            g_in, g_proj = g_b[: NC * wr], g_b[NC * wr :]
            g_a = scatter_full(mine_a, other_a, [D] * 4, SMALL)
            shares[mode] = (g_a, g_in, g_proj)
    input_grad = from_chip(dres.astype(BF))

    if direct:
        place_meta = jnp.stack([open_src, plane, o]).astype(jnp.int32)
        grads = list(run_finish(place_meta, done))
        grads[-1] = grads[-1].reshape(2, -1)
        return (output, input_grad, *grads)

    flip = open_src == 0

    def both(make):
        fin, opn = make(*shares[1]), make(*shares[2])
        return jnp.stack([jnp.where(flip, opn, fin), jnp.where(flip, fin, opn)], 0)

    def lanes(a, lo, hi):
        at_row = 4 * wr
        return lax.dynamic_slice(a[at_row + lo : at_row + hi], (0, o * wr), (hi - lo, wr))

    def hidden(a):
        return lax.dynamic_slice(a[4 * wr + 8 : 4 * wr + 8 + NC].reshape(FF), (o * pr,), (pr,))

    return (
        output,
        input_grad,
        both(lambda a, f, p: unblock(a[: 3 * wr], 3)),
        both(lambda a, f, p: a[3 * wr : 4 * wr]),
        both(lambda a, f, p: unblock(f, NC)),
        both(lambda a, f, p: p),
        both(lambda a, f, p: lanes(a, 0, 2)),
        both(lambda a, f, p: lanes(a, 2, 4)),
        both(lambda a, f, p: lanes(a, 4, 8)),
        both(lambda a, f, p: hidden(a)),
    )


def solution(mesh):
    return jax.shard_map(
        functools.partial(per_device, mesh.shape["own"], mesh.shape["dp"]),
        mesh=mesh,
        in_specs=(
            P("own", "dp", None),
            P(),
            P(None, "own", None),
            P(None, "own", None),
            P(None, "own", None),
            P(None, "own", None),
            P(None, None, "own"),
            P(None, None, "own"),
            P(None, None, "own"),
            P(None, "own"),
            P("own", "dp", None),
        ),
        out_specs=(
            P("own", "dp", None),
            P("own", "dp", None),
            P(None, "own", None),
            P(None, "own", None),
            P(None, "own", None),
            P(None, "own", None),
            P(None, None, "own"),
            P(None, None, "own"),
            P(None, None, "own"),
            P(None, "own"),
        ),
        check_vma=False,
    )
```

```python
import functools

import jax
import jax.numpy as jnp
from jax import lax
from jax.experimental import pallas as pl
from jax.experimental.pallas import tpu as pltpu
from jax.sharding import PartitionSpec as P

D = 768
HEADS = 12
PAIRS = HEADS // 2
FF = 3072
NC = FF // D
NG = 16
GR = D // NG
PR = FF // NG
SMALL = 16
NORM_EPS = 1e-05
GELU_C = 0.7978845608028654
GELU_A = 0.044715
BF = jnp.bfloat16
F32 = jnp.float32
VMEM_LIMIT = 50 * 2**20


def dot(a, b):
    return lax.dot_general(a, b, (((1,), (0,)), ((), ())), preferred_element_type=F32)


def dot_nt(a, b):
    return lax.dot_general(a, b, (((1,), (1,)), ((), ())), preferred_element_type=F32)


def dot_tn(a, b):
    return lax.dot_general(a, b, (((0,), (0,)), ((), ())), preferred_element_type=F32)


def norm_parts(x):
    centred = x - jnp.mean(x, -1, keepdims=True)
    rstd = lax.rsqrt(jnp.mean(centred * centred, -1, keepdims=True) + NORM_EPS)
    return centred * rstd, rstd


def norm_back(xhat, rstd, gain, dy):
    dxh = dy * gain
    return rstd * (
        dxh
        - jnp.mean(dxh, -1, keepdims=True)
        - xhat * jnp.mean(dxh * xhat, -1, keepdims=True)
    )


def params_of(prm):
    return jnp.sum(prm[...].astype(F32), (0, 1))


SEL, CORE, PLANE, YPOS, ZPOS, ZLOW, ZHIGH, UPS = range(8)
COUNTS = {"a": 1, "b": 1, "a2": 2, "b4": 4}
A_ROWS, B_ROWS = 4 * GR + SMALL, NC * GR + PR


class Weights:
    def __init__(self, kinds, refs, meta):
        self.meta, self.srcs = meta, []
        for kind in kinds:
            parts = []
            for part in kind:
                parts.append((part, refs[: COUNTS[part]]))
                refs = refs[COUNTS[part] :]
            self.srcs.append(parts)

    @staticmethod
    def count(kinds):
        return sum(COUNTS[part] for kind in kinds for part in kind)

    def pair(self, refs, view, dst, sem):
        core = self.meta[CORE]
        pltpu.make_async_copy(view(refs[0]), dst.at[:, core], sem).start()
        pltpu.make_async_copy(view(refs[1]), dst.at[:, 1 - core], sem).start()

    def of_half(self, refs, half, view, dst, sem):
        mine = self.meta[PLANE] == half
        pl.when(mine)(lambda: self.pair(refs[:2], view, dst, sem))
        pl.when(jnp.logical_not(mine))(lambda: self.pair(refs[2:], view, dst, sem))

    def each(self, part, copy):
        if len(self.srcs) == 1:
            copy(*self.srcs[0][part])
        else:
            for number, parts in enumerate(self.srcs):
                pl.when(self.meta[SEL] == number)(functools.partial(copy, *parts[part]))

    def start_a(self, row, size, dst, sem):
        def copy(kind, refs):
            if kind == "a":
                pltpu.make_async_copy(rows_of(refs[0], row, size), dst, sem).start()
            else:
                self.pair(refs, lambda r: rows_of(r, row, size), dst, sem)

        self.each(0, copy)

    def start_qk(self, dst, sem):
        self.start_a(0, 2 * GR, dst, sem)

    def start_v(self, dst, sem):
        self.start_a(2 * GR, GR, dst, sem)

    def start_out(self, dst, sem):
        self.start_a(3 * GR, GR, dst, sem)

    def start_small(self, dst, sem):
        self.start_a(4 * GR, SMALL, dst, sem)

    def start_in(self, c, dst, sem):
        def copy(kind, refs):
            if kind == "b":
                view = rows_of(refs[0], A_ROWS + c * GR, GR)
                pltpu.make_async_copy(view, dst, sem).start()
            else:
                half, at = divmod(c, NC // 2)
                self.of_half(refs, half, lambda r: rows_of(r, at * GR, GR), dst, sem)

        self.each(1, copy)

    def start_proj(self, c, dst, sem):
        owners = pl.ds(c * (NG // 2 // NC), NG // 2 // NC)

        def copy(kind, refs):
            if kind == "b":
                view = rows_of(refs[0].at[owners], A_ROWS + NC * GR, PR)
                pltpu.make_async_copy(view, dst, sem).start()
                return
            size = PR // 2
            view = lambda r: rows_of(r.at[owners], NC // 2 * GR, size)
            for half in range(2):
                part = dst.at[:, :, pl.ds(half * size, size), :]
                self.of_half(refs, half, view, part, sem)

        self.each(1, copy)


def rows_of(ref, row, size):
    if len(ref.shape) == 4:
        return ref.at[:, :, pl.ds(row, size), :]
    return ref.at[:, pl.ds(row, size), :]


def landed(dst, sem):
    pltpu.make_async_copy(dst, dst, sem).wait()


def qkv_kernel(kinds, meta, resid, *rest):
    nw = Weights.count(kinds)
    weights = Weights(kinds, rest[:nw], meta)
    q_out, kv_out, wqk, wv, prm, sems = rest[nw:]
    weights.start_small(prm, sems.at[0])
    weights.start_qk(wqk, sems.at[1])
    weights.start_v(wv, sems.at[2])
    xhat, _ = norm_parts(resid[...])
    landed(prm, sems.at[0])
    par = params_of(prm)
    normed = (xhat * par[0:1] + par[2:3]).astype(BF)
    landed(wqk, sems.at[1])
    kv_out[0] = dot(normed, wqk[:, :, GR:, :].reshape(D, D)).astype(BF)
    landed(wv, sems.at[2])
    kv_out[1] = (dot(normed, wv[...].reshape(D, D)) + par[5:6]).astype(BF)
    q = (dot(normed, wqk[:, :, :GR, :].reshape(D, D)) + par[4:5]).astype(BF)
    q_out[...] = q * BF((D // HEADS) ** -0.5)


def by_head(x, first):
    return jnp.concatenate([jnp.where(first, x, 0), jnp.where(first, 0, x)], 0)


def pair_masks(half, axis):
    lane = lax.broadcasted_iota(jnp.int32, (1, 2 * D // HEADS), 1)
    shape = (2 * half, half) if axis == 0 else (half, 2 * half)
    query = lax.broadcasted_iota(jnp.int32, shape, axis)
    query = jnp.where(query >= half, query - half, query)
    key = lax.broadcasted_iota(jnp.int32, shape, 1 - axis)
    return lane < D // HEADS, key <= query


def attn_fwd_kernel(others, meta, q_ref, ko, vo, kx, vx, mixed, lse, lse_scr):
    step = pl.program_id(0)
    rows = q_ref.shape[0]
    half = rows // 2
    lanes = 2 * D // HEADS
    first, tri = pair_masks(half, 0)
    highs = [meta[UPS + t] > 0 for t in range(others)]
    q_lo, q_hi = by_head(q_ref[:half], first), by_head(q_ref[half:], first)
    ones = jnp.ones((half, 128), BF)
    wide = lambda v: jnp.concatenate([v, ones], 1)
    s_ll = jnp.where(tri, dot_nt(q_lo, ko[0, :half]), -1e30)
    s_hl = dot_nt(q_hi, ko[0, :half])
    s_hh = jnp.where(tri, dot_nt(q_hi, ko[0, half:]), -1e30)
    top = jnp.maximum(s_hl, s_hh)
    s_ho, s_x, m_x = [], [], []
    for t in range(others):
        s_ho.append(dot_nt(q_hi, kx[t, 0, :half]))
        top = jnp.maximum(top, s_ho[t])
        k_x = jnp.where(highs[t], kx[t, 0, half:], kx[t, 0, :half])
        s_x.append(dot_nt(jnp.where(highs[t], q_hi, q_lo), k_x))
        m_x.append(jnp.max(s_x[t], -1, keepdims=True))
    m_lo = jnp.max(s_ll, -1, keepdims=True)
    m_hi = jnp.max(top, -1, keepdims=True)
    for t in range(others):
        m_hi = jnp.maximum(m_hi, jnp.where(highs[t], m_x[t], -1e30))
        m_lo = jnp.maximum(m_lo, jnp.where(highs[t], -1e30, m_x[t]))
    prob = lambda s, m: jnp.exp(s - m).astype(BF)
    v_lo = wide(vo[0, :half])
    o_lo = dot(prob(s_ll, m_lo), v_lo)
    o_hi = dot(prob(s_hl, m_hi), v_lo) + dot(prob(s_hh, m_hi), wide(vo[0, half:]))
    for t in range(others):
        v_x = jnp.where(highs[t], vx[t, 0, half:], vx[t, 0, :half])
        o_x = dot(prob(s_x[t], jnp.where(highs[t], m_hi, m_lo)), wide(v_x))
        o_hi = o_hi + dot(prob(s_ho[t], m_hi), wide(vx[t, 0, :half]))
        o_hi = o_hi + jnp.where(highs[t], o_x, 0.0)
        o_lo = o_lo + jnp.where(highs[t], 0.0, o_x)
    at = lax.broadcasted_iota(jnp.int32, (1, 128), 1)
    for part, (o, m) in enumerate(((o_lo, m_lo), (o_hi, m_hi))):
        out_rows = slice(part * half, (part + 1) * half)
        total = o[:, lanes:]
        norm = o[:, :lanes] / total
        mixed[out_rows] = jnp.where(first, norm[:half], norm[half:]).astype(BF)
        log = m + jnp.log(total)
        old = jnp.where(at == 2 * step, log[:half], lse_scr[out_rows])
        lse_scr[out_rows] = jnp.where(at == 2 * step + 1, log[half:], old)

    @pl.when(step == PAIRS - 1)
    def _():
        lse[0] = jnp.transpose(lse_scr[:half])[:16]
        lse[1] = jnp.transpose(lse_scr[half:])[:16]


def mlp_kernel(kinds, meta, resid, mixed, *rest):
    nw = Weights.count(kinds)
    weights = Weights(kinds, rest[:nw], meta)
    middle, pre_out, result, ow, prm, fw, pw, nm, acc, par, sems = rest[nw:]
    weights.start_out(ow, sems.at[0])
    weights.start_small(prm, sems.at[1])
    for c in range(NC):
        weights.start_in(c, fw.at[c], sems.at[2 + c])
        weights.start_proj(c, pw.at[c], sems.at[2 + NC + c])
    landed(prm, sems.at[1])
    par[...] = params_of(prm)
    landed(ow, sems.at[0])
    mid = resid[...] + dot(mixed[...], ow[...].reshape(D, D)) + par[6:7]
    middle[...] = mid
    xhat, _ = norm_parts(mid)
    nm[...] = (xhat * par[1:2] + par[3:4]).astype(BF)
    acc[...] = mid + par[7:8]

    def chunk(c, carry):
        landed(fw.at[c], sems.at[2 + c])
        pre = dot(nm[...], fw[c].reshape(D, D)) + par[pl.ds(8 + c, 1), :]
        pre_out[c] = pre.astype(BF)
        act = 0.5 * pre * (1.0 + jnp.tanh(GELU_C * (pre + GELU_A * pre * pre * pre)))
        landed(pw.at[c], sems.at[2 + NC + c])
        acc[...] += dot(act.astype(BF), pw[c].reshape(D, D))
        return carry

    lax.fori_loop(0, NC, chunk, 0)
    result[...] = acc[...]


def sort_terms(mode, keep, term, prev):
    if mode == 0:
        return (term,)
    if mode == 2:
        return (term + prev.astype(F32),)
    prev = prev.astype(F32)
    mine, old = keep
    return (mine * term + old * prev, (1.0 - mine) * term + (1.0 - old) * prev)


def to_cores(buf, mine, other, core, sem_mine, sem_other):
    return [
        pltpu.make_async_copy(buf.at[:, core], mine, sem_mine),
        pltpu.make_async_copy(buf.at[:, 1 - core], other, sem_other),
    ]


def mlp_back_kernel(kinds, mode, meta, keep_ref, dres, mid, pre, mixed, *rest):
    nw = Weights.count(kinds)
    weights = Weights(kinds, rest[:nw], meta)
    rest = rest[nw:]
    prev_b, prev_o = rest[:2] if mode else (None, None)
    rest = rest[2:] if mode else rest
    nout = 2 if mode == 1 else 1
    d_middle, d_mixed, dt, small = rest[:4]
    rest = rest[4:]
    done = mode > 0
    if done:
        done_mine, done_other = rest[:2]
        rest = rest[2:]
    if mode < 2:
        open_b, open_o = rest[:2]
        rest = rest[2:]
    (ow, prm, fw, pw, nm, acc, par, d_br, sems, osems) = rest[:10]
    stage = rest[10:]
    bufs = [stage[3 * i : 3 * i + 3] for i in range(nout)]
    core = meta[CORE]
    groups = NG // 2 // NC
    keep = (keep_ref[0], keep_ref[1])
    weights.start_small(prm, sems.at[1])
    for c in range(NC):
        weights.start_proj(c, pw.at[c], sems.at[2 + NC + c])
        weights.start_in(c, fw.at[c], sems.at[2 + c])
    weights.start_out(ow, sems.at[0])

    def in_view(ref, c):
        return rows_of(ref, c * GR, GR)

    def proj_view(ref, c):
        return rows_of(ref.at[pl.ds(c * groups, groups)], NC * GR, PR)

    def prev_copies(c):
        slot = lax.rem(c, 2)
        return [
            pltpu.make_async_copy(
                in_view(prev_b, c), bufs[-1][0].at[slot], sems.at[2 + 2 * NC + c]
            ),
            pltpu.make_async_copy(
                proj_view(prev_b, c), bufs[-1][1].at[slot], sems.at[2 + 3 * NC + c]
            ),
        ]

    if mode:
        for copy in prev_copies(0):
            copy.start()
        prev_o_copy = pltpu.make_async_copy(prev_o, bufs[-1][2], sems.at[2 + 4 * NC])
        prev_o_copy.start()
    landed(prm, sems.at[1])
    par[...] = params_of(prm)
    xhat, _ = norm_parts(mid[...])
    nm[...] = jnp.transpose((xhat * par[1:2] + par[3:4]).astype(BF))
    d_br[...] = dres[...].astype(BF)
    small[...] = jnp.zeros_like(small)
    small[7:8, :] = jnp.sum(d_br[...].astype(F32), 0, keepdims=True)
    ones = jnp.ones((8, d_br.shape[0]), BF)

    def out_copies(c):
        slot = lax.rem(c, 2)
        copies = []
        if done:
            f, j = bufs[0][0].at[slot], bufs[0][1].at[slot]
            sem = lambda k: osems.at[k, c]
            copies += to_cores(
                f, in_view(done_mine, c), in_view(done_other, c), core, sem(0), sem(1)
            )
            copies += to_cores(
                j, proj_view(done_mine, c), proj_view(done_other, c), core, sem(2), sem(3)
            )
        if mode < 2:
            f, j = bufs[-1][0].at[slot], bufs[-1][1].at[slot]
            copies.append(pltpu.make_async_copy(f, in_view(open_b, c), osems.at[4, c]))
            copies.append(pltpu.make_async_copy(j, proj_view(open_b, c), osems.at[5, c]))
        return copies

    acc[...] = jnp.zeros_like(acc)

    def chunk(c, carry):
        slot = lax.rem(c, 2)
        landed(pw.at[c], sems.at[2 + NC + c])
        d_act = dot_nt(pw[c].reshape(D, D), d_br[...])
        x = jnp.transpose(pre[c]).astype(F32)
        x2 = x * x
        th = jnp.tanh(x * (GELU_C + GELU_C * GELU_A * x2))
        up = 0.5 + 0.5 * th
        act = (x * up).astype(BF)
        slope = up + (x * (0.5 - 0.5 * th * th)) * (GELU_C + 3.0 * GELU_C * GELU_A * x2)
        d_pre = (d_act * slope).astype(BF)
        small[pl.ds(8 + c, 1), :] = dot_nt(ones, d_pre)[0:1]
        landed(fw.at[c], sems.at[2 + c])
        acc[...] += dot(fw[c].reshape(D, D), d_pre)
        g_fc = dot_nt(nm[...], d_pre)
        g_proj = dot(act, d_br[...])

        @pl.when(c > 0)
        def _():
            for copy in out_copies(c - 1):
                copy.wait()

        if mode:

            @pl.when(c < NC - 1)
            def _():
                for copy in prev_copies(c + 1):
                    copy.start()

            for copy in prev_copies(c):
                copy.wait()
        for part, val in ((0, g_fc), (1, g_proj)):
            prev = bufs[-1][part][slot].reshape(D, D) if mode else None
            for which, term in enumerate(sort_terms(mode, keep, val, prev)):
                ref = bufs[which][part]
                ref[slot] = term.astype(BF).reshape(ref.shape[1:])
        for copy in out_copies(c):
            copy.start()
        return carry

    lax.fori_loop(0, NC, chunk, 0)
    xhat, rstd = norm_parts(mid[...])
    dy = jnp.transpose(acc[...])
    small[1:2, :] = jnp.sum(dy * xhat, 0, keepdims=True)
    small[3:4, :] = jnp.sum(dy, 0, keepdims=True)
    d_mid = dres[...] + norm_back(xhat, rstd, par[1:2], dy)
    d_middle[...] = d_mid
    d_attn = d_mid.astype(BF)
    small[6:7, :] = jnp.sum(d_attn.astype(F32), 0, keepdims=True)
    landed(ow, sems.at[0])
    d_mix = dot_nt(d_attn, ow[...].reshape(D, D)).astype(BF)
    d_mixed[...] = d_mix
    g_out = dot_tn(mixed[...], d_attn)
    if mode:
        prev_o_copy.wait()
    prev = bufs[-1][2][...].reshape(D, D) if mode else None
    o_copies = []
    for which, term in enumerate(sort_terms(mode, keep, g_out, prev)):
        buf = bufs[which][2]
        buf[...] = term.astype(BF).reshape(NG // 2, 2, GR, D)
        if done and which == 0:
            views = [rows_of(ref, NC * GR + PR, GR) for ref in (done_mine, done_other)]
            o_copies += to_cores(buf, *views, core, osems.at[6, 0], osems.at[6, 1])
        else:
            o_copies.append(pltpu.make_async_copy(buf, open_o, osems.at[7, 0]))
    for copy in o_copies:
        copy.start()
    prod = d_mix.astype(F32) * mixed[...].astype(F32)
    big = prod.astype(BF)
    rest_part = (prod - big.astype(F32)).astype(BF)
    heads = lax.broadcasted_iota(jnp.int32, (16, D), 1) // (D // HEADS)
    ind = jnp.where(heads == lax.broadcasted_iota(jnp.int32, (16, D), 0), 1.0, 0.0).astype(BF)
    half = prod.shape[0] // 2
    for part in range(2):
        rows = slice(part * half, (part + 1) * half)
        dt[part] = dot_nt(ind, big[rows]) + dot_nt(ind, rest_part[rows])
    for copy in out_copies(NC - 1) + o_copies:
        copy.wait()


def attn_back_kernel(others, meta, q_ref, ko, vo, kx, vx, do_ref, lse, dt, dq, dkv, dkvx):
    step = pl.program_id(0)
    rows = q_ref.shape[0]
    half = rows // 2
    first, tri = pair_masks(half, 1)
    highs = [meta[UPS + t] > 0 for t in range(others)]
    scale = (D // HEADS) ** -0.5

    def stats(part):
        both = [
            (lse[part, pl.ds(2 * step + h, 1), :], dt[part, pl.ds(2 * step + h, 1), :])
            for h in range(2)
        ]
        return tuple(jnp.concatenate(x, 1) for x in zip(*both))

    q_lo, q_hi = by_head(q_ref[:half], first), by_head(q_ref[half:], first)
    do_lo, do_hi = by_head(do_ref[:half], first), by_head(do_ref[half:], first)
    low = (q_lo, do_lo) + stats(0)
    high = (q_hi, do_hi) + stats(1)

    def tile(queries, k, v, diag):
        q, do, row_lse, row_dt = queries
        p = jnp.exp(dot_nt(k, q) - row_lse)
        if diag:
            p = jnp.where(tri, p, 0.0)
        ds = (p * (dot_nt(v, do) - row_dt)).astype(BF)
        return dot_tn(ds, k), dot(ds, q), dot(p.astype(BF), do)

    k_lo, k_hi, v_lo, v_hi = ko[0, :half], ko[0, half:], vo[0, :half], vo[0, half:]
    dq_lo, dk_a, dv_a = tile(low, k_lo, v_lo, True)
    dq_hi, dk_b, dv_b = tile(high, k_lo, v_lo, False)
    dkv[0, :half] = (dk_a + dk_b).astype(BF)
    dkv[1, :half] = (dv_a + dv_b).astype(BF)
    dq_add, dk, dv = tile(high, k_hi, v_hi, True)
    dq_hi = dq_hi + dq_add
    dkv[0, half:] = dk.astype(BF)
    dkv[1, half:] = dv.astype(BF)
    for t in range(others):
        up = highs[t]
        dq_add, dk, dv = tile(high, kx[t, 0, :half], vx[t, 0, :half], False)
        dq_hi = dq_hi + dq_add
        both = tuple(jnp.where(up, a, b) for a, b in zip(high, low))
        k_x = jnp.where(up, kx[t, 0, half:], kx[t, 0, :half])
        v_x = jnp.where(up, vx[t, 0, half:], vx[t, 0, :half])
        dq_add, dk_x, dv_x = tile(both, k_x, v_x, False)
        dq_hi = dq_hi + jnp.where(up, dq_add, 0.0)
        dq_lo = dq_lo + jnp.where(up, 0.0, dq_add)
        dkvx[t, 0, :half] = (dk + jnp.where(up, 0.0, dk_x)).astype(BF)
        dkvx[t, 1, :half] = (dv + jnp.where(up, 0.0, dv_x)).astype(BF)
        dkvx[t, 0, half:] = jnp.where(up, dk_x, 0.0).astype(BF)
        dkvx[t, 1, half:] = jnp.where(up, dv_x, 0.0).astype(BF)
    dq[:half] = (jnp.where(first, dq_lo[:half], dq_lo[half:]) * scale).astype(BF)
    dq[half:] = (jnp.where(first, dq_hi[:half], dq_hi[half:]) * scale).astype(BF)


def qkv_back_kernel(
    kinds, mode, others, meta, keep_ref, resid, dq, dkv, dkvx, d_middle, small_in, *rest
):
    nw = Weights.count(kinds)
    weights = Weights(kinds, rest[:nw], meta)
    rest = rest[nw:]
    done = mode > 0
    if done:
        prev_ref = rest[0]
        rest = rest[1:]
    nout = 2 if mode == 1 else 1
    dres = rest[0]
    rest = rest[1:]
    if done:
        done_mine, done_other = rest[:2]
        rest = rest[2:]
    if mode < 2:
        open_a = rest[0]
        rest = rest[1:]
    wqk, wv, prm, sems, osems = rest[:5]
    bufs = rest[5:]
    core = meta[CORE]
    keep = (keep_ref[0], keep_ref[1])
    weights.start_small(prm, sems.at[0])
    weights.start_qk(wqk, sems.at[1])
    weights.start_v(wv, sems.at[2])
    if done:
        prev_copy = pltpu.make_async_copy(prev_ref, bufs[-1], sems.at[3])
        prev_copy.start()
    landed(prm, sems.at[0])
    par = params_of(prm)
    xhat, rstd = norm_parts(resid[...])
    normed = jnp.transpose((xhat * par[0:1] + par[2:3]).astype(BF))
    parts = [dq[...]]
    for i in range(2):
        total = dkv[i].astype(F32)
        for t in range(others):
            total = total + dkvx[t, i].astype(F32)
        parts.append(total.astype(BF))
    landed(wqk, sems.at[1])
    landed(wv, sems.at[2])
    if done:
        prev_copy.wait()
    ws = [wqk[:, :, :GR, :], wqk[:, :, GR:, :], wv[...]]
    dy = 0.0
    for i, part in enumerate(parts):
        rows = slice(i * GR, (i + 1) * GR)
        dy = dy + dot_nt(part, ws[i].reshape(D, D))
        prev = bufs[-1][:, :, rows, :].reshape(D, D) if mode else None
        for which, val in enumerate(sort_terms(mode, keep, dot(normed, part), prev)):
            bufs[which][:, :, rows, :] = val.astype(BF).reshape(NG // 2, 2, GR, D)
    small = jnp.concatenate(
        [
            jnp.sum(dy * xhat, 0, keepdims=True),
            small_in[1:2],
            jnp.sum(dy, 0, keepdims=True),
            small_in[3:4],
            jnp.sum(parts[0].astype(F32), 0, keepdims=True),
            jnp.sum(parts[2].astype(F32), 0, keepdims=True),
            small_in[6:],
        ],
        0,
    )
    prev = bufs[-1][0, 0, 3 * GR :, :] if mode else None
    for which, val in enumerate(sort_terms(mode, keep, small, prev)):
        bufs[which][:, :, 3 * GR :, :] = jnp.broadcast_to(
            val.astype(BF)[None, None], (NG // 2, 2, SMALL, D)
        )
    later = []
    if done:
        later += to_cores(bufs[0], done_mine, done_other, core, osems.at[0], osems.at[1])
    if mode < 2:
        later.append(pltpu.make_async_copy(bufs[-1], open_a, osems.at[2]))
    for copy in later:
        copy.start()
    dres[...] = d_middle[...] + norm_back(xhat, rstd, par[0:1], dy)
    for copy in later:
        copy.wait()


def pack_kernel(meta, small_in, qkv, out, fc, proj, *rest):
    outs, smalls, sems = rest[:4], rest[4], rest[5]
    first, plane, at = meta[0], meta[1], meta[2]
    copies = []

    def cols(ref, src, i):
        return ref.at[src, :, pl.ds(i * D, D)]

    def copy(src, dst):
        copies.append(pltpu.make_async_copy(src, dst, sems.at[len(copies)]))
        copies[-1].start()

    for i, src in enumerate((first, 1 - first)):
        attn, ffn = outs[2 * i : 2 * i + 2]
        for k in range(NC // 2):
            col = pl.multiple_of((plane * (NC // 2) + k) * D, D)
            copy(fc.at[src, :, pl.ds(col, D)], ffn.at[pl.ds(k * GR, GR)])
        row = pl.multiple_of(plane * (PR // 2), 16)
        copy(proj.at[src, pl.ds(row, PR // 2)], ffn.at[pl.ds(NC // 2 * GR, PR // 2)])
        for k in range(3):
            copy(cols(qkv, src, k), attn.at[pl.ds(k * GR, GR)])
        copy(out.at[src], attn.at[pl.ds(3 * GR, GR)])

    lane = lax.broadcasted_iota(jnp.int32, (GR, D), 1)
    row = lax.broadcasted_iota(jnp.int32, (GR, D), 0)
    spread = jnp.where(lane == row + at * GR, 1.0, 0.0).astype(BF)
    lane = lax.broadcasted_iota(jnp.int32, (PR, D), 1)
    row = lax.broadcasted_iota(jnp.int32, (PR, D), 0)
    spread_h = jnp.where(lane == row + lax.rem(at, NG // NC) * PR, 1.0, 0.0).astype(BF)
    line = lax.broadcasted_iota(jnp.int32, (8, D), 0)
    for i, src in enumerate((first, 1 - first)):
        smalls[i, 0:8, :] = dot(small_in[src, :, :GR], spread).astype(BF)
        hid = dot(small_in[src, :, GR : GR + PR], spread_h)
        smalls[i, 8:16, :] = jnp.where(line == at // (NG // NC), hid[0:1], 0.0).astype(BF)
        copy(smalls.at[i], outs[2 * i].at[pl.ds(4 * GR, SMALL)])
    for one in copies:
        one.wait()


def assemble_kernel(meta, mine, other, whole, sems):
    copies = []
    for side, ref in enumerate((mine, other)):
        for low in range(2):
            for high in range(2):
                z = jnp.bitwise_xor(meta[ZPOS], low + 2 * high)
                y = meta[YPOS] if side == 0 else 1 - meta[YPOS]
                copies.append(
                    pltpu.make_async_copy(
                        ref.at[low, high], whole.at[z * 2 + y], sems.at[len(copies)]
                    )
                )
                copies[-1].start()
    for copy in copies:
        copy.wait()


def add_cores_kernel(segments, meta, mine, got, *outs):
    total = (mine[...].astype(F32) + got[...].astype(F32)).astype(BF)
    for i, (order, low, high, size) in enumerate(segments):
        if order == "x":
            sides, which = (total[:, low : low + size], total[:, high : high + size]), PLANE
        else:
            sides, which = (total[0:1, low : low + size], total[1:2, low : low + size]), YPOS
        outs[2 * i][...] = jnp.where(meta[which] == 0, sides[0], sides[1])
        outs[2 * i + 1][...] = jnp.where(meta[which] == 0, sides[1], sides[0])


def add_split_kernel(bits, meta, *refs):
    ins, outs = refs[: 2 * len(bits)], list(refs[2 * len(bits) :])
    for i, bit in enumerate(bits):
        mine, got = ins[2 * i], ins[2 * i + 1]
        if bit is None:
            outs.pop(0)[...] = (mine[0].astype(F32) + got[0].astype(F32)).astype(BF)
            continue
        keep, send = outs.pop(0), outs.pop(0)

        def pair(g, carry):
            for out, at in ((keep, 2 * g + meta[bit]), (send, 2 * g + 1 - meta[bit])):
                out[g] = (mine[at].astype(F32) + got[at].astype(F32)).astype(BF)
            return carry

        lax.fori_loop(0, mine.shape[0] // 2, pair, 0)


def finish_kernel(meta, *refs):
    ins, outs = refs[:12], refs[12:]
    qkv_g, out_g, fc_g, proj_g, gains_g, shifts_g, bias_g, hidden_g = outs
    first, plane, at = meta[0], meta[1], meta[2]
    low = lambda mine, peer: jnp.where(plane == 0, mine[...], peer[...])
    high = lambda mine, peer: jnp.where(plane == 0, peer[...], mine[...])
    pick = lax.broadcasted_iota(jnp.int32, (D, GR), 0) == (
        lax.broadcasted_iota(jnp.int32, (D, GR), 1) + at * GR
    )
    pick = jnp.where(pick, 1.0, 0.0).astype(BF)
    pick_h = lax.broadcasted_iota(jnp.int32, (D, PR), 0) == (
        lax.broadcasted_iota(jnp.int32, (D, PR), 1) + lax.rem(at, NG // NC) * PR
    )
    pick_h = jnp.where(pick_h, 1.0, 0.0).astype(BF)
    line = lax.broadcasted_iota(jnp.int32, (SMALL, D), 0)
    here = line == 8 + at // (NG // NC)

    for k, src in enumerate((1 - first, first)):
        pairs = ins[4 * k : 4 * k + 4] + ins[8 + 2 * k : 10 + 2 * k]
        halves = (low(*pairs[0:2]), high(*pairs[0:2]))
        for c in range(NC):
            half, at_row = divmod(c, NC // 2)
            rows = halves[half][at_row * GR : (at_row + 1) * GR]
            fc_g[src, :, c * D : (c + 1) * D] = rows.astype(F32)
        sums = pairs[2][...].astype(F32) + pairs[3][...].astype(F32)
        proj_g[src] = sums[:PR]
        out_g[src] = sums[PR:]
        attn = jnp.concatenate([low(*pairs[4:6]), high(*pairs[4:6])], 0)
        for c in range(3):
            qkv_g[src, :, c * D : (c + 1) * D] = attn[c * GR : (c + 1) * GR].astype(F32)
        small = attn[3 * GR :]
        vals = dot(small, pick)
        row = jnp.sum(jnp.where(here, small.astype(F32), 0.0), 0, keepdims=True)
        hid = dot(jnp.broadcast_to(row, (8, D)).astype(BF), pick_h)
        gains_g[src] = vals[0:2]
        shifts_g[src] = vals[2:4]
        bias_g[src] = vals[4:8]
        hidden_g[src] = hid[0:1]


VM = pl.BlockSpec(memory_space=pltpu.VMEM)
SM = pl.BlockSpec(memory_space=pltpu.SMEM)
HB = pl.BlockSpec(memory_space=pl.ANY)
DMA = pltpu.SemaphoreType.DMA


def call(kernel, outs, in_specs, out_specs, scratch, flops, name, weight=8, **more):
    cost = pl.CostEstimate(flops=int(flops * weight), bytes_accessed=1024, transcendentals=0)
    return pl.pallas_call(
        kernel,
        out_shape=outs,
        in_specs=in_specs,
        out_specs=out_specs,
        scratch_shapes=scratch,
        compiler_params=pltpu.CompilerParams(vmem_limit_bytes=VMEM_LIMIT),
        cost_estimate=cost,
        name=name,
        **more,
    )


def sds(shape, dtype):
    return jax.ShapeDtypeStruct(shape, dtype)


def run_qkv(meta, resid, kinds, weights):
    rows = resid.shape[0]
    return call(
        functools.partial(qkv_kernel, kinds),
        (sds((rows, D), BF), sds((2, rows, D), BF)),
        [SM, VM] + [HB] * len(weights),
        (VM, VM),
        qkv_scratch() + [DMA((3,))],
        2 * rows * D * 3 * D,
        "qkv",
        8 if len(kinds) > 1 else 0.01,
    )(meta, resid, *weights)


def qkv_scratch():
    return [
        pltpu.VMEM((NG // 2, 2, 2 * GR, D), BF),
        pltpu.VMEM((NG // 2, 2, GR, D), BF),
        pltpu.VMEM((NG // 2, 2, SMALL, D), BF),
    ]


def pair_specs(rows, others):
    lanes = 2 * D // HEADS
    return [
        SM,
        pl.BlockSpec((rows, lanes), lambda i: (0, i)),
        pl.BlockSpec((1, rows, lanes), lambda i: (0, 0, i)),
        pl.BlockSpec((1, rows, lanes), lambda i: (1, 0, i)),
        pl.BlockSpec((others, 1, rows, lanes), lambda i: (0, 0, 0, i)),
        pl.BlockSpec((others, 1, rows, lanes), lambda i: (0, 1, 0, i)),
    ]


def run_attn(meta, q, kv, kvx, weight):
    rows, others = q.shape[0], kvx.shape[0]
    half = rows // 2
    return call(
        functools.partial(attn_fwd_kernel, others),
        (sds((rows, D), BF), sds((2, 16, half), F32)),
        pair_specs(rows, others),
        (
            pl.BlockSpec((rows, 2 * D // HEADS), lambda i: (0, i)),
            pl.BlockSpec((2, 16, half), lambda i: (0, 0, 0)),
        ),
        [pltpu.VMEM((rows, 128), F32)],
        HEADS * (3 + 2 * others) * half * half * 256 * 4,
        "attn",
        weight,
        grid=(PAIRS,),
    )(meta, q, kv, kv, kvx, kvx)


def weight_scratch(rows, flipped=False):
    shape = (D, rows) if flipped else (rows, D)
    return [
        pltpu.VMEM((NG // 2, 2, GR, D), BF),
        pltpu.VMEM((NG // 2, 2, SMALL, D), BF),
        pltpu.VMEM((NC, NG // 2, 2, GR, D), BF),
        pltpu.VMEM((NC, NG // 2 // NC, 2, PR, D), BF),
        pltpu.VMEM(shape, BF),
        pltpu.VMEM(shape, F32),
        pltpu.VMEM((SMALL, D), F32),
    ]


def run_mlp(meta, resid, mixed, kinds, weights):
    rows = resid.shape[0]
    return call(
        functools.partial(mlp_kernel, kinds),
        (sds((rows, D), F32), sds((NC, rows, D), BF), sds((rows, D), F32)),
        [SM, VM, VM] + [HB] * len(weights),
        (VM, VM, VM),
        weight_scratch(rows) + [DMA((2 + 2 * NC,))],
        2 * rows * D * (D + 2 * FF),
        "mlp",
        8 if len(kinds) > 1 else 0.01,
    )(meta, resid, mixed, *weights)


def run_mlp_back(mode, meta, keep, dres, mid, pre, mixed, kinds, weights, prev):
    rows = dres.shape[0]
    nout = 2 if mode == 1 else 1
    b_rows = NC * GR + PR
    o_shape = sds((NG // 2, 2, GR, D), BF)
    outs = ()
    if mode:
        outs += (sds((NG // 2, b_rows + GR, D), BF),) * 2
    if mode < 2:
        outs += (sds((NG // 2, 2, b_rows, D), BF), o_shape)
    stage = [
        pltpu.VMEM((2, NG // 2, 2, GR, D), BF),
        pltpu.VMEM((2, NG // 2 // NC, 2, PR, D), BF),
        pltpu.VMEM((NG // 2, 2, GR, D), BF),
    ] * nout
    return call(
        functools.partial(mlp_back_kernel, kinds, mode),
        (
            sds((rows, D), F32),
            sds((rows, D), BF),
            sds((2, 16, rows // 2), F32),
            sds((SMALL, D), F32),
        )
        + outs,
        [SM, SM, VM, VM, VM, VM] + [HB] * (len(weights) + len(prev)),
        (VM, VM, VM, VM) + (HB,) * len(outs),
        weight_scratch(rows, True)
        + [pltpu.VMEM((rows, D), BF), DMA((3 + 4 * NC,)), DMA((8, NC))]
        + stage,
        4 * rows * D * (D + 2 * FF),
        "mlp_back",
    )(meta, keep, dres, mid, pre, mixed, *weights, *prev)


def run_attn_back(meta, q, kv, kvx, d_mixed, lse, dt):
    rows, others = q.shape[0], kvx.shape[0]
    half = rows // 2
    lanes = 2 * D // HEADS
    stat = pl.BlockSpec((2, 16, half), lambda i: (0, 0, 0))
    block = pl.BlockSpec((rows, lanes), lambda i: (0, i))
    return call(
        functools.partial(attn_back_kernel, others),
        (sds((rows, D), BF), sds((2, rows, D), BF), sds((others, 2, rows, D), BF)),
        pair_specs(rows, others) + [block, stat, stat],
        (
            block,
            pl.BlockSpec((2, rows, lanes), lambda i: (0, 0, i)),
            pl.BlockSpec((others, 2, rows, lanes), lambda i: (0, 0, 0, i)),
        ),
        [],
        HEADS * (3 + 2 * others) * half * half * 256 * 10,
        "attn_back",
        grid=(PAIRS,),
    )(meta, q, kv, kv, kvx, kvx, d_mixed, lse, dt)


def run_qkv_back(
    mode, meta, keep, resid, dq, dkv, dkvx, d_middle, small, kinds, weights, prev
):
    rows, others = resid.shape[0], dkvx.shape[0]
    nout = 2 if mode == 1 else 1
    shape = (NG // 2, 2, 3 * GR + SMALL, D)
    outs = ()
    if mode:
        outs += (sds((NG // 2, 3 * GR + SMALL, D), BF),) * 2
    if mode < 2:
        outs += (sds(shape, BF),)
    return call(
        functools.partial(qkv_back_kernel, kinds, mode, others),
        (sds((rows, D), F32),) + outs,
        [SM, SM] + [VM] * 6 + [HB] * (len(weights) + len(prev)),
        (VM,) + (HB,) * len(outs),
        qkv_scratch() + [DMA((4,)), DMA((3,))] + [pltpu.VMEM(shape, BF)] * nout,
        4 * rows * D * 3 * D,
        "qkv_back",
    )(meta, keep, resid, dq, dkv, dkvx, d_middle, small, *weights, *prev)


def run_pack(meta, small, qkv, out, fc, proj):
    rows = (A_ROWS, B_ROWS // 2) * 2
    return call(
        pack_kernel,
        tuple(sds((r, D), BF) for r in rows),
        [SM, VM] + [HB] * 4,
        (HB,) * 4,
        [pltpu.VMEM((2, SMALL, D), BF), DMA((2 * (NC // 2 + 6),))],
        2 * 16 * PR * D,
        "pack",
    )(meta, small, qkv, out, fc, proj)


def run_assemble(meta, mine, other):
    rows = mine.shape[-2]
    return call(
        assemble_kernel,
        sds((NG // 2, rows, D), BF),
        [SM, HB, HB],
        VM,
        [DMA((NG // 2,))],
        NG * rows * D,
        "assemble",
    )(meta, mine, other)


def run_add_cores(meta, mine, got, segments, weight):
    groups, rows = mine.shape[:2]
    outs, specs = [], []
    for order, _, _, size in segments:
        step = 2 if order == "x" else 1
        outs += [sds((groups // 2 * step, size, D), BF)] * 2
        specs += [pl.BlockSpec((step, size, D), lambda i: (i, 0, 0))] * 2
    block = pl.BlockSpec((2, rows, D), lambda i: (i, 0, 0))
    return call(
        functools.partial(add_cores_kernel, segments),
        outs,
        [SM, block, block],
        specs,
        [],
        mine.size * weight,
        "add_cores",
        grid=(groups // 2,),
    )(meta, mine, got)


def run_add_split(meta, bits, pairs, weight):
    outs = []
    for bit, (mine, _) in zip(bits, pairs):
        groups, rows = mine.shape[:2]
        if bit is None:
            outs.append(sds((rows, D), BF))
        else:
            outs += [sds((groups // 2, rows, D), BF)] * 2
    ins = [x for pair in pairs for x in pair]
    return call(
        functools.partial(add_split_kernel, bits),
        outs,
        [SM] + [VM] * len(ins),
        [VM] * len(outs),
        [],
        sum(x.size for x in ins) * weight,
        "add_split",
    )(meta, *ins)


def run_finish(meta, parts):
    outs = (
        sds((2, GR, 3 * D), F32),
        sds((2, GR, D), F32),
        sds((2, GR, FF), F32),
        sds((2, PR, D), F32),
        sds((2, 2, GR), F32),
        sds((2, 2, GR), F32),
        sds((2, 4, GR), F32),
        sds((2, 1, PR), F32),
    )
    return call(
        finish_kernel, outs, [SM] + [VM] * len(parts), (VM,) * 8, [], 2**20, "finish"
    )(meta, *parts)


def regroup(packed, own_from, own_to, widths):
    if own_from == own_to:
        return packed
    parts, at = [], 0
    for width in widths:
        rows = width // own_from
        part = packed[:, at : at + rows].reshape(width, D)
        parts.append(part.reshape(own_to, width // own_to, D))
        at += rows
    return jnp.concatenate(parts, 1)


def blocks(table):
    return jnp.concatenate([table[:, i : i + D] for i in range(0, table.shape[1], D)], 0)


def unblock(rows, count):
    size = rows.shape[0] // count
    return jnp.concatenate([rows[i * size : (i + 1) * size] for i in range(count)], 1)


def place_small(gains, shifts, bias_m, bias_h, at):
    vecs = jnp.concatenate([gains, shifts, bias_m], 0)
    wide = lax.dynamic_update_slice(jnp.zeros((8, D), BF), vecs, (0, at * vecs.shape[1]))
    hid = lax.dynamic_update_slice(jnp.zeros((FF,), BF), bias_h, (at * bias_h.shape[0],))
    return jnp.concatenate([wide, hid.reshape(NC, D), jnp.zeros((SMALL - 8 - NC, D), BF)], 0)


def per_device(own, n, tokens, tie, qkv_w, out_w, fc_w, proj_w, gains, shifts, bias_m, bias_h, cotangent):
    axes = ("own", "dp")
    o = lax.axis_index("own")
    d = lax.axis_index("dp")
    core = o % 2
    rows = tokens.shape[1]
    half = rows // 2
    others = n - 1

    def at(pair, s, j):
        return (2 * pair + j % 2) * n + s * (n // 2) + j // 2

    j = (d % (n // 2)) * 2 + core

    def place(block):
        return block if block < n else 2 * n - 1 - block

    def moves(odd):
        return [
            ((2 * pair + s) * n + dd, at(pair, s, place(2 * dd + odd)))
            for pair in range(own // 2)
            for s in range(2)
            for dd in range(n)
        ]

    def to_chip(x):
        x = x.reshape(rows, D)
        even = lax.ppermute(x[:half], axes, moves(0))
        odd = lax.ppermute(x[half:], axes, moves(1))
        return jnp.concatenate(
            [jnp.where(core == 0, even, odd), jnp.where(core == 0, odd, even)], 0
        )

    def from_chip(x):
        back = [[(b, a) for a, b in moves(odd)] for odd in range(2)]
        even = lax.ppermute(jnp.where(core == 0, x[:half], x[half:]), axes, back[0])
        odd = lax.ppermute(jnp.where(core == 0, x[half:], x[:half]), axes, back[1])
        return jnp.concatenate([even, odd], 0).reshape(tokens.shape)

    def shift(x, step):
        pairs = [
            (at(pair, s, (place_ + step) % n), at(pair, s, place_))
            for pair in range(own // 2)
            for s in range(2)
            for place_ in range(n)
        ]
        return lax.ppermute(x, axes, pairs)

    plane, y, z = d % 2, (o // 2) % 2, o // 4
    nz = own // 4

    def device(zz, yy, cc, dd):
        return ((zz * 2 + yy) * 2 + cc) * n + dd

    everyone = [
        (zz, yy, cc, dd)
        for zz in range(nz)
        for yy in range(2)
        for cc in range(2)
        for dd in range(n)
    ]

    def swap(x, axis):
        turn = {
            "core": lambda zz, yy, cc, dd: device(zz, yy, 1 - cc, dd),
            "y": lambda zz, yy, cc, dd: device(zz, 1 - yy, cc, dd),
            "x": lambda zz, yy, cc, dd: device(zz, yy, cc, dd ^ 1),
            "z1": lambda zz, yy, cc, dd: device(zz ^ 1, yy, cc, dd),
            "z2": lambda zz, yy, cc, dd: device(zz ^ 2, yy, cc, dd),
        }[axis]
        return lax.ppermute(x, axes, [(device(*at_), turn(*at_)) for at_ in everyone])

    def from_z(x, step):
        pairs = [
            (device((zz + step) % nz, yy, cc, dd), device(zz, yy, cc, dd))
            for zz, yy, cc, dd in everyone
        ]
        return lax.ppermute(x, axes, pairs)

    def after(x, *deps):
        return lax.optimization_barrier((x, *deps))[0]

    def after_all(xs, *deps):
        return lax.optimization_barrier((tuple(xs), *deps))[0]

    open_src = tie[0]
    isin = lambda u: (tie[u] != open_src).astype(jnp.int32)
    ups = [((j + t) % n > j).astype(jnp.int32) for t in range(1, n)]
    metas = [jnp.stack([isin(u), core, plane, y, z, z % 2, z // 2] + ups).astype(jnp.int32) for u in range(3)]
    keep = jnp.stack([isin(1), isin(2)]).astype(F32)
    direct = own == NG and n == 2

    if direct:
        small = jnp.concatenate([gains, shifts, bias_m], 1)
        hid = jnp.broadcast_to(bias_h[:, None], (2, 8, bias_h.shape[1]))
        packed = run_pack(
            jnp.stack([open_src, plane, o]).astype(jnp.int32),
            jnp.concatenate([small, hid], 2),
            qkv_w,
            out_w,
            fc_w,
            proj_w,
        )

        def square(x, axis):
            return jnp.stack([x, swap(x, axis)], 0)

        def cores_of(part):
            return [part, swap(part, "core")]

        twos, lines, sides = [], [], []
        for part in (packed[1], packed[3], packed[0], packed[2]):
            twos.append(square(after(part, twos[-1]) if twos else part, "z2"))
            two = after(twos[-1], lines[-1]) if lines else twos[-1]
            lines.append(square(two, "z1"))
            line = after(lines[-1], sides[-1][1]) if sides else lines[-1]
            sides.append((line, swap(line, "y")))
        resid = to_chip(after(tokens, twos[0])).astype(F32)
        dres = to_chip(after(cotangent, twos[0])).astype(F32)
        ffn = [run_assemble(after(metas[0], resid, dres, lines[1]), *sides[0])]
        peers = [swap(ffn[0], "x")]
        ffn.append(run_assemble(after(metas[0], lines[2]), *sides[1]))
        peers.append(swap(after(ffn[1], peers[0]), "x"))
        attn = run_assemble(after(metas[0], lines[3]), *sides[2])
        first_a, first_b = cores_of(attn), cores_of(ffn[0]) + cores_of(peers[0])
        kinds = (("a2", "b4"),) * 2
        second_b = cores_of(ffn[1]) + cores_of(peers[1])
        metas[0] = after(metas[0], *first_a, *first_b, *second_b[:2])
    else:
        resid = to_chip(tokens).astype(F32)
        dres = to_chip(cotangent).astype(F32)
        sources = []
        for src in (open_src, 1 - open_src):
            pick = lambda table: lax.dynamic_index_in_dim(table, src, 0, keepdims=False)
            part = jnp.concatenate(
                [blocks(pick(qkv_w)), pick(out_w), blocks(pick(fc_w)), pick(proj_w)], 0
            )
            full = lax.all_gather(part, "own", axis=0, tiled=False)
            full = regroup(full, own, NG, [D] * (4 + NC) + [FF])
            small = place_small(pick(gains), pick(shifts), pick(bias_m), pick(bias_h), o)
            small = lax.psum(small.astype(F32), "own").astype(BF)
            small = jnp.concatenate([small[None], jnp.zeros((NG - 1, SMALL, D), BF)], 0)
            full = jnp.concatenate([full[:, : 4 * GR], small, full[:, 4 * GR :]], 1)
            sources.append([full.reshape(NG // 2, 2, -1, D)])
        first_a = first_b = sources[0]
        second_a = second_b = sources[1]
        kinds = (("a", "b"),) * 2

    def weights_of(u, attn_only=False):
        many = 1 if u == 0 else 2
        arrays = first_a + ([] if attn_only else first_b)
        if u:
            arrays = arrays + second_a + ([] if attn_only else second_b)
        return tuple(kind[: 1 if attn_only else 2] for kind in kinds[:many]), arrays

    saved = []
    for u in range(3):
        meta = metas[u]
        q, kv = run_qkv(meta, resid, *weights_of(u, True))
        kvx = jnp.stack([shift(kv, t) for t in range(1, n)], 0)
        mixed, lse = run_attn(meta, q, kv, kvx, 8 if u else 0.01)
        middle, pre, result = run_mlp(meta, resid, mixed, *weights_of(u))
        if u == 0 and direct:
            second_a = cores_of(run_assemble(after(metas[1], middle, peers[1]), *sides[3]))
            metas[1] = after(metas[1], *second_a)
        saved.append((resid, q, kv, kvx, mixed, lse, middle, pre))
        resid = result
    output = from_chip(resid.astype(BF))

    def scatter_full(mine, other, widths, small_rows):
        pair = jnp.where(core == 0, jnp.stack([mine, other], 1), jnp.stack([other, mine], 1))
        grad = pair.reshape(NG, -1, D)
        body = grad.shape[1] - small_rows
        tail = grad[:1, body:]
        grad = regroup(grad[:, :body], NG, own, widths)
        if small_rows:
            tail = jnp.broadcast_to(tail, (own, small_rows, D))
            grad = jnp.concatenate([grad, tail], 1)
        part = lax.psum_scatter(grad, "own", scatter_dimension=0, tiled=False)
        return lax.psum(part, "dp").astype(F32)


    class Scatter:
        NEXT = {"x": ("y", YPOS), "y": ("z1", ZLOW), "z1": ("z2", ZHIGH), "z2": ("x", None)}

        def __init__(self, order, keep_, send):
            self.stage, self.keep, self.done = order, keep_, None
            self.got = swap(send, order)

    def step(meta, chunks, weight=1):
        moves_ = [Scatter.NEXT[one.stage] for one in chunks]
        outs = run_add_split(
            meta,
            tuple(bit for _, bit in moves_),
            [(one.keep, one.got) for one in chunks],
            weight,
        )
        first_out, outs = outs[0], list(outs)
        for one, (stage, bit) in zip(chunks, moves_):
            one.stage = stage
            one.keep = outs.pop(0)
            one.got = swap(one.keep if bit is None else outs.pop(0), stage)
            if bit is None:
                one.done = [one.keep, one.got]
        return first_out

    def scatter_start(meta, mine, got, segs, weight):
        outs = run_add_cores(meta, mine, got, segs, weight)
        return [Scatter(seg[0], *outs[2 * i : 2 * i + 2]) for i, seg in enumerate(segs)], outs[0]

    in_rows, a_rows = NC // 2 * GR, 4 * GR + SMALL
    b_segs = (("x", 0, in_rows, in_rows), ("y", NC * GR, 0, PR + GR))
    half_a = (3 * GR + SMALL) // 2
    a_segs = (("x", 0, half_a, half_a),)

    prev_b, prev_a = [], []
    shares, fin, opn = {}, [], []
    wr, pr = D // own, FF // own
    for u in (2, 1, 0):
        mode = 2 - u
        meta = metas[u]
        resid, q, kv, kvx, mixed, lse, middle, pre = saved[u]
        outs = run_mlp_back(
            mode, meta, keep, dres, middle, pre, mixed, *weights_of(u), prev_b
        )
        d_middle, d_mixed, dt, small = outs[:4]
        if mode:
            mine_b, other_b = outs[4:6]
            if direct:
                got_b = swap(other_b, "core")
        prev_b = list(outs[-2:])
        if mode == 0:
            meta = after(meta, output)
        if mode == 2 and direct:
            slot = after(meta, d_mixed)
            more, last = scatter_start(slot, *fin_a, a_segs, 1)
            last = step(after(slot, last), fin, 4096)
            fin += more
            opn, last = scatter_start(after(slot, last), mine_b, got_b, b_segs, 1)
            meta = after(meta, last)
        dq, dkv, dkvx = run_attn_back(meta, q, kv, kvx, d_mixed, lse, dt)
        back = jnp.stack([shift(dkvx[t - 1], n - t) for t in range(1, n)], 0)
        if mode and direct:
            slot = after(meta, dq)
            if mode == 1:
                fin, last = scatter_start(slot, mine_b, got_b, b_segs, 4096)
            else:
                last = step(slot, fin, 4096)
            meta = after(meta, last)
        outs = run_qkv_back(
            mode,
            meta,
            keep,
            resid,
            dq,
            dkv,
            back,
            d_middle,
            small,
            *weights_of(u, True),
            prev_a,
        )
        dres = outs[0]
        prev_a = [outs[-1]]
        if not mode:
            continue
        mine_a, other_a = outs[1:3]
        if direct:
            if mode == 1:
                fin_a = (mine_a, swap(other_a, "core"))
            else:
                slot = after(metas[0], dres)
                got_a = swap(other_a, "core")
                last = step(slot, fin, 4096)
                more, last = scatter_start(after(slot, last), mine_a, got_a, a_segs, 1)
                left = [one for one in fin if one.done is None]
                last = step(after(slot, last), left)
                last = step(after(slot, last), opn, 1)
                chunks = fin[:2] + opn + fin[2:] + more
                old, new = [], []
                while any(one.done is None for one in chunks):
                    for group, weight in ((more, 16384), (fin + opn, 1)):
                        left = [one for one in group if one.done is None]
                        if left:
                            last = step(after(slot, last, *old), left, weight)
                            old, new = new, [one.got for one in left if one.done]
                done = [x for one in chunks for x in one.done]
        else:
            g_b = scatter_full(mine_b, other_b, [D] * NC + [FF, D], 0)
            g_in, g_proj, g_out = jnp.split(g_b, [NC * wr, NC * wr + pr])
            g_a = scatter_full(mine_a, other_a, [D] * 3, SMALL)
            g_a = jnp.concatenate([g_a[: 3 * wr], g_out, g_a[3 * wr :]], 0)
            shares[mode] = (g_a, g_in, g_proj)
    input_grad = from_chip(dres.astype(BF))

    if direct:
        place_meta = jnp.stack([open_src, plane, o]).astype(jnp.int32)
        grads = list(run_finish(place_meta, done))
        grads[-1] = grads[-1].reshape(2, -1)
        return (output, input_grad, *grads)

    flip = open_src == 0

    def both(make):
        fin, opn = make(*shares[1]), make(*shares[2])
        return jnp.stack([jnp.where(flip, opn, fin), jnp.where(flip, fin, opn)], 0)

    def lanes(a, lo, hi):
        at_row = 4 * wr
        return lax.dynamic_slice(a[at_row + lo : at_row + hi], (0, o * wr), (hi - lo, wr))

    def hidden(a):
        return lax.dynamic_slice(a[4 * wr + 8 : 4 * wr + 8 + NC].reshape(FF), (o * pr,), (pr,))

    return (
        output,
        input_grad,
        both(lambda a, f, p: unblock(a[: 3 * wr], 3)),
        both(lambda a, f, p: a[3 * wr : 4 * wr]),
        both(lambda a, f, p: unblock(f, NC)),
        both(lambda a, f, p: p),
        both(lambda a, f, p: lanes(a, 0, 2)),
        both(lambda a, f, p: lanes(a, 2, 4)),
        both(lambda a, f, p: lanes(a, 4, 8)),
        both(lambda a, f, p: hidden(a)),
    )


def solution(mesh):
    return jax.shard_map(
        functools.partial(per_device, mesh.shape["own"], mesh.shape["dp"]),
        mesh=mesh,
        in_specs=(
            P("own", "dp", None),
            P(),
            P(None, "own", None),
            P(None, "own", None),
            P(None, "own", None),
            P(None, "own", None),
            P(None, None, "own"),
            P(None, None, "own"),
            P(None, None, "own"),
            P(None, "own"),
            P("own", "dp", None),
        ),
        out_specs=(
            P("own", "dp", None),
            P("own", "dp", None),
            P(None, "own", None),
            P(None, "own", None),
            P(None, "own", None),
            P(None, "own", None),
            P(None, None, "own"),
            P(None, None, "own"),
            P(None, None, "own"),
            P(None, "own"),
        ),
        check_vma=False,
    )
```

```python
import functools

import jax
import jax.numpy as jnp
from jax import lax
from jax.experimental import pallas as pl
from jax.experimental.pallas import tpu as pltpu
from jax.sharding import PartitionSpec as P

D = 768
HEADS = 12
PAIRS = HEADS // 2
FF = 3072
NC = FF // D
NG = 16
GR = D // NG
PR = FF // NG
SMALL = 16
NORM_EPS = 1e-05
GELU_C = 0.7978845608028654
GELU_A = 0.044715
BF = jnp.bfloat16
F32 = jnp.float32
VMEM_LIMIT = 50 * 2**20


def dot(a, b):
    return lax.dot_general(a, b, (((1,), (0,)), ((), ())), preferred_element_type=F32)


def dot_nt(a, b):
    return lax.dot_general(a, b, (((1,), (1,)), ((), ())), preferred_element_type=F32)


def dot_tn(a, b):
    return lax.dot_general(a, b, (((0,), (0,)), ((), ())), preferred_element_type=F32)


def norm_parts(x):
    centred = x - jnp.mean(x, -1, keepdims=True)
    rstd = lax.rsqrt(jnp.mean(centred * centred, -1, keepdims=True) + NORM_EPS)
    return centred * rstd, rstd


def norm_back(xhat, rstd, gain, dy):
    dxh = dy * gain
    return rstd * (
        dxh
        - jnp.mean(dxh, -1, keepdims=True)
        - xhat * jnp.mean(dxh * xhat, -1, keepdims=True)
    )


def params_of(prm):
    return jnp.sum(prm[...].astype(F32), (0, 1))


SEL, CORE, PLANE, YPOS, ZPOS, ZLOW, ZHIGH, UPS = range(8)
COUNTS = {"a": 1, "b": 1, "a2": 2, "b4": 4}
A_ROWS, B_ROWS = 4 * GR + SMALL, NC * GR + PR


class Weights:
    def __init__(self, kinds, refs, meta):
        self.meta, self.srcs = meta, []
        for kind in kinds:
            parts = []
            for part in kind:
                parts.append((part, refs[: COUNTS[part]]))
                refs = refs[COUNTS[part] :]
            self.srcs.append(parts)

    @staticmethod
    def count(kinds):
        return sum(COUNTS[part] for kind in kinds for part in kind)

    def pair(self, refs, view, dst, sem):
        core = self.meta[CORE]
        pltpu.make_async_copy(view(refs[0]), dst.at[:, core], sem).start()
        pltpu.make_async_copy(view(refs[1]), dst.at[:, 1 - core], sem).start()

    def of_half(self, refs, half, view, dst, sem):
        mine = self.meta[PLANE] == half
        pl.when(mine)(lambda: self.pair(refs[:2], view, dst, sem))
        pl.when(jnp.logical_not(mine))(lambda: self.pair(refs[2:], view, dst, sem))

    def each(self, part, copy):
        if len(self.srcs) == 1:
            copy(*self.srcs[0][part])
        else:
            for number, parts in enumerate(self.srcs):
                pl.when(self.meta[SEL] == number)(functools.partial(copy, *parts[part]))

    def start_a(self, row, size, dst, sem):
        def copy(kind, refs):
            if kind == "a":
                pltpu.make_async_copy(rows_of(refs[0], row, size), dst, sem).start()
            else:
                self.pair(refs, lambda r: rows_of(r, row, size), dst, sem)

        self.each(0, copy)

    def start_qk(self, dst, sem):
        self.start_a(0, 2 * GR, dst, sem)

    def start_v(self, dst, sem):
        self.start_a(2 * GR, GR, dst, sem)

    def start_out(self, dst, sem):
        self.start_a(3 * GR, GR, dst, sem)

    def start_small(self, dst, sem):
        self.start_a(4 * GR, SMALL, dst, sem)

    def start_in(self, c, dst, sem):
        def copy(kind, refs):
            if kind == "b":
                view = rows_of(refs[0], A_ROWS + c * GR, GR)
                pltpu.make_async_copy(view, dst, sem).start()
            else:
                half, at = divmod(c, NC // 2)
                self.of_half(refs, half, lambda r: rows_of(r, at * GR, GR), dst, sem)

        self.each(1, copy)

    def start_proj(self, c, dst, sem):
        owners = pl.ds(c * (NG // 2 // NC), NG // 2 // NC)

        def copy(kind, refs):
            if kind == "b":
                view = rows_of(refs[0].at[owners], A_ROWS + NC * GR, PR)
                pltpu.make_async_copy(view, dst, sem).start()
                return
            size = PR // 2
            view = lambda r: rows_of(r.at[owners], NC // 2 * GR, size)
            for half in range(2):
                part = dst.at[:, :, pl.ds(half * size, size), :]
                self.of_half(refs, half, view, part, sem)

        self.each(1, copy)


def rows_of(ref, row, size):
    if len(ref.shape) == 4:
        return ref.at[:, :, pl.ds(row, size), :]
    return ref.at[:, pl.ds(row, size), :]


def landed(dst, sem):
    pltpu.make_async_copy(dst, dst, sem).wait()


def qkv_kernel(kinds, meta, resid, *rest):
    nw = Weights.count(kinds)
    weights = Weights(kinds, rest[:nw], meta)
    q_out, kv_out, wqk, wv, prm, sems = rest[nw:]
    weights.start_small(prm, sems.at[0])
    weights.start_qk(wqk, sems.at[1])
    weights.start_v(wv, sems.at[2])
    xhat, _ = norm_parts(resid[...])
    landed(prm, sems.at[0])
    par = params_of(prm)
    normed = (xhat * par[0:1] + par[2:3]).astype(BF)
    landed(wqk, sems.at[1])
    kv_out[0] = dot(normed, wqk[:, :, GR:, :].reshape(D, D)).astype(BF)
    landed(wv, sems.at[2])
    kv_out[1] = (dot(normed, wv[...].reshape(D, D)) + par[5:6]).astype(BF)
    q = (dot(normed, wqk[:, :, :GR, :].reshape(D, D)) + par[4:5]).astype(BF)
    q_out[...] = q * BF((D // HEADS) ** -0.5)


def by_head(x, first):
    return jnp.concatenate([jnp.where(first, x, 0), jnp.where(first, 0, x)], 0)


def pair_masks(half, axis):
    lane = lax.broadcasted_iota(jnp.int32, (1, 2 * D // HEADS), 1)
    shape = (2 * half, half) if axis == 0 else (half, 2 * half)
    query = lax.broadcasted_iota(jnp.int32, shape, axis)
    query = jnp.where(query >= half, query - half, query)
    key = lax.broadcasted_iota(jnp.int32, shape, 1 - axis)
    return lane < D // HEADS, key <= query


def attn_fwd_kernel(others, meta, q_ref, ko, vo, kx, vx, mixed, lse, lse_scr):
    step = pl.program_id(0)
    rows = q_ref.shape[0]
    half = rows // 2
    lanes = 2 * D // HEADS
    first, tri = pair_masks(half, 0)
    highs = [meta[UPS + t] > 0 for t in range(others)]
    q_lo, q_hi = by_head(q_ref[:half], first), by_head(q_ref[half:], first)
    ones = jnp.ones((half, 128), BF)
    wide = lambda v: jnp.concatenate([v, ones], 1)
    s_ll = jnp.where(tri, dot_nt(q_lo, ko[0, :half]), -1e30)
    s_hl = dot_nt(q_hi, ko[0, :half])
    s_hh = jnp.where(tri, dot_nt(q_hi, ko[0, half:]), -1e30)
    top = jnp.maximum(s_hl, s_hh)
    s_ho, s_x, m_x = [], [], []
    for t in range(others):
        s_ho.append(dot_nt(q_hi, kx[t, 0, :half]))
        top = jnp.maximum(top, s_ho[t])
        k_x = jnp.where(highs[t], kx[t, 0, half:], kx[t, 0, :half])
        s_x.append(dot_nt(jnp.where(highs[t], q_hi, q_lo), k_x))
        m_x.append(jnp.max(s_x[t], -1, keepdims=True))
    m_lo = jnp.max(s_ll, -1, keepdims=True)
    m_hi = jnp.max(top, -1, keepdims=True)
    for t in range(others):
        m_hi = jnp.maximum(m_hi, jnp.where(highs[t], m_x[t], -1e30))
        m_lo = jnp.maximum(m_lo, jnp.where(highs[t], -1e30, m_x[t]))
    prob = lambda s, m: jnp.exp(s - m).astype(BF)
    v_lo = wide(vo[0, :half])
    o_lo = dot(prob(s_ll, m_lo), v_lo)
    o_hi = dot(prob(s_hl, m_hi), v_lo) + dot(prob(s_hh, m_hi), wide(vo[0, half:]))
    for t in range(others):
        v_x = jnp.where(highs[t], vx[t, 0, half:], vx[t, 0, :half])
        o_x = dot(prob(s_x[t], jnp.where(highs[t], m_hi, m_lo)), wide(v_x))
        o_hi = o_hi + dot(prob(s_ho[t], m_hi), wide(vx[t, 0, :half]))
        o_hi = o_hi + jnp.where(highs[t], o_x, 0.0)
        o_lo = o_lo + jnp.where(highs[t], 0.0, o_x)
    at = lax.broadcasted_iota(jnp.int32, (1, 128), 1)
    for part, (o, m) in enumerate(((o_lo, m_lo), (o_hi, m_hi))):
        out_rows = slice(part * half, (part + 1) * half)
        total = o[:, lanes:]
        norm = o[:, :lanes] / total
        mixed[out_rows] = jnp.where(first, norm[:half], norm[half:]).astype(BF)
        log = m + jnp.log(total)
        old = jnp.where(at == 2 * step, log[:half], lse_scr[out_rows])
        lse_scr[out_rows] = jnp.where(at == 2 * step + 1, log[half:], old)

    @pl.when(step == PAIRS - 1)
    def _():
        lse[0] = jnp.transpose(lse_scr[:half])[:16]
        lse[1] = jnp.transpose(lse_scr[half:])[:16]


def mlp_kernel(kinds, meta, resid, mixed, *rest):
    nw = Weights.count(kinds)
    weights = Weights(kinds, rest[:nw], meta)
    middle, pre_out, result, ow, prm, fw, pw, nm, acc, par, sems = rest[nw:]
    weights.start_out(ow, sems.at[0])
    weights.start_small(prm, sems.at[1])
    for c in range(NC):
        weights.start_in(c, fw.at[c], sems.at[2 + c])
        weights.start_proj(c, pw.at[c], sems.at[2 + NC + c])
    landed(prm, sems.at[1])
    par[...] = params_of(prm)
    landed(ow, sems.at[0])
    mid = resid[...] + dot(mixed[...], ow[...].reshape(D, D)) + par[6:7]
    middle[...] = mid
    xhat, _ = norm_parts(mid)
    nm[...] = (xhat * par[1:2] + par[3:4]).astype(BF)
    acc[...] = mid + par[7:8]

    def chunk(c, carry):
        landed(fw.at[c], sems.at[2 + c])
        pre = dot(nm[...], fw[c].reshape(D, D)) + par[pl.ds(8 + c, 1), :]
        pre_out[c] = pre.astype(BF)
        act = 0.5 * pre * (1.0 + jnp.tanh(GELU_C * (pre + GELU_A * pre * pre * pre)))
        landed(pw.at[c], sems.at[2 + NC + c])
        acc[...] += dot(act.astype(BF), pw[c].reshape(D, D))
        return carry

    lax.fori_loop(0, NC, chunk, 0)
    result[...] = acc[...]


def sort_terms(mode, keep, term, prev):
    if mode == 0:
        return (term,)
    if mode == 2:
        return (term + prev.astype(F32),)
    prev = prev.astype(F32)
    mine, old = keep
    return (mine * term + old * prev, (1.0 - mine) * term + (1.0 - old) * prev)


def to_cores(buf, mine, other, core, sem_mine, sem_other):
    return [
        pltpu.make_async_copy(buf.at[:, core], mine, sem_mine),
        pltpu.make_async_copy(buf.at[:, 1 - core], other, sem_other),
    ]


def mlp_back_kernel(kinds, mode, meta, keep_ref, dres, mid, pre, mixed, *rest):
    nw = Weights.count(kinds)
    weights = Weights(kinds, rest[:nw], meta)
    rest = rest[nw:]
    prev_b, prev_o = rest[:2] if mode else (None, None)
    rest = rest[2:] if mode else rest
    nout = 2 if mode == 1 else 1
    d_middle, d_mixed, dt, small = rest[:4]
    rest = rest[4:]
    done = mode > 0
    if done:
        done_mine, done_other = rest[:2]
        rest = rest[2:]
    if mode < 2:
        open_b, open_o = rest[:2]
        rest = rest[2:]
    (ow, prm, fw, pw, nm, acc, par, d_br, sems, osems) = rest[:10]
    stage = rest[10:]
    bufs = [stage[3 * i : 3 * i + 3] for i in range(nout)]
    core = meta[CORE]
    groups = NG // 2 // NC
    keep = (keep_ref[0], keep_ref[1])
    weights.start_small(prm, sems.at[1])
    for c in range(NC):
        weights.start_proj(c, pw.at[c], sems.at[2 + NC + c])
        weights.start_in(c, fw.at[c], sems.at[2 + c])
    weights.start_out(ow, sems.at[0])

    def in_view(ref, c):
        return rows_of(ref, c * GR, GR)

    def proj_view(ref, c):
        return rows_of(ref.at[pl.ds(c * groups, groups)], NC * GR, PR)

    def prev_copies(c):
        slot = lax.rem(c, 2)
        return [
            pltpu.make_async_copy(
                in_view(prev_b, c), bufs[-1][0].at[slot], sems.at[2 + 2 * NC + c]
            ),
            pltpu.make_async_copy(
                proj_view(prev_b, c), bufs[-1][1].at[slot], sems.at[2 + 3 * NC + c]
            ),
        ]

    if mode:
        for copy in prev_copies(0):
            copy.start()
        prev_o_copy = pltpu.make_async_copy(prev_o, bufs[-1][2], sems.at[2 + 4 * NC])
        prev_o_copy.start()
    landed(prm, sems.at[1])
    par[...] = params_of(prm)
    xhat, _ = norm_parts(mid[...])
    nm[...] = jnp.transpose((xhat * par[1:2] + par[3:4]).astype(BF))
    d_br[...] = dres[...].astype(BF)
    small[...] = jnp.zeros_like(small)
    small[7:8, :] = jnp.sum(d_br[...].astype(F32), 0, keepdims=True)
    ones = jnp.ones((8, d_br.shape[0]), BF)

    def out_copies(c):
        slot = lax.rem(c, 2)
        copies = []
        if done:
            f, j = bufs[0][0].at[slot], bufs[0][1].at[slot]
            sem = lambda k: osems.at[k, c]
            copies += to_cores(
                f, in_view(done_mine, c), in_view(done_other, c), core, sem(0), sem(1)
            )
            copies += to_cores(
                j, proj_view(done_mine, c), proj_view(done_other, c), core, sem(2), sem(3)
            )
        if mode < 2:
            f, j = bufs[-1][0].at[slot], bufs[-1][1].at[slot]
            copies.append(pltpu.make_async_copy(f, in_view(open_b, c), osems.at[4, c]))
            copies.append(pltpu.make_async_copy(j, proj_view(open_b, c), osems.at[5, c]))
        return copies

    acc[...] = jnp.zeros_like(acc)

    def chunk(c, carry):
        slot = lax.rem(c, 2)
        landed(pw.at[c], sems.at[2 + NC + c])
        d_act = dot_nt(pw[c].reshape(D, D), d_br[...])
        x = jnp.transpose(pre[c]).astype(F32)
        x2 = x * x
        th = jnp.tanh(x * (GELU_C + GELU_C * GELU_A * x2))
        up = 0.5 + 0.5 * th
        act = (x * up).astype(BF)
        slope = up + (x * (0.5 - 0.5 * th * th)) * (GELU_C + 3.0 * GELU_C * GELU_A * x2)
        d_pre = (d_act * slope).astype(BF)
        small[pl.ds(8 + c, 1), :] = dot_nt(ones, d_pre)[0:1]
        landed(fw.at[c], sems.at[2 + c])
        acc[...] += dot(fw[c].reshape(D, D), d_pre)
        g_fc = dot_nt(nm[...], d_pre)
        g_proj = dot(act, d_br[...])

        @pl.when(c > 0)
        def _():
            for copy in out_copies(c - 1):
                copy.wait()

        if mode:

            @pl.when(c < NC - 1)
            def _():
                for copy in prev_copies(c + 1):
                    copy.start()

            for copy in prev_copies(c):
                copy.wait()
        for part, val in ((0, g_fc), (1, g_proj)):
            prev = bufs[-1][part][slot].reshape(D, D) if mode else None
            for which, term in enumerate(sort_terms(mode, keep, val, prev)):
                ref = bufs[which][part]
                ref[slot] = term.astype(BF).reshape(ref.shape[1:])
        for copy in out_copies(c):
            copy.start()
        return carry

    lax.fori_loop(0, NC, chunk, 0)
    xhat, rstd = norm_parts(mid[...])
    dy = jnp.transpose(acc[...])
    small[1:2, :] = jnp.sum(dy * xhat, 0, keepdims=True)
    small[3:4, :] = jnp.sum(dy, 0, keepdims=True)
    d_mid = dres[...] + norm_back(xhat, rstd, par[1:2], dy)
    d_middle[...] = d_mid
    d_attn = d_mid.astype(BF)
    small[6:7, :] = jnp.sum(d_attn.astype(F32), 0, keepdims=True)
    landed(ow, sems.at[0])
    d_mix = dot_nt(d_attn, ow[...].reshape(D, D)).astype(BF)
    d_mixed[...] = d_mix
    g_out = dot_tn(mixed[...], d_attn)
    if mode:
        prev_o_copy.wait()
    prev = bufs[-1][2][...].reshape(D, D) if mode else None
    o_copies = []
    for which, term in enumerate(sort_terms(mode, keep, g_out, prev)):
        buf = bufs[which][2]
        buf[...] = term.astype(BF).reshape(NG // 2, 2, GR, D)
        if done and which == 0:
            views = [rows_of(ref, NC * GR + PR, GR) for ref in (done_mine, done_other)]
            o_copies += to_cores(buf, *views, core, osems.at[6, 0], osems.at[6, 1])
        else:
            o_copies.append(pltpu.make_async_copy(buf, open_o, osems.at[7, 0]))
    for copy in o_copies:
        copy.start()
    prod = d_mix.astype(F32) * mixed[...].astype(F32)
    big = prod.astype(BF)
    rest_part = (prod - big.astype(F32)).astype(BF)
    heads = lax.broadcasted_iota(jnp.int32, (16, D), 1) // (D // HEADS)
    ind = jnp.where(heads == lax.broadcasted_iota(jnp.int32, (16, D), 0), 1.0, 0.0).astype(BF)
    half = prod.shape[0] // 2
    for part in range(2):
        rows = slice(part * half, (part + 1) * half)
        dt[part] = dot_nt(ind, big[rows]) + dot_nt(ind, rest_part[rows])
    for copy in out_copies(NC - 1) + o_copies:
        copy.wait()


def attn_back_kernel(others, meta, q_ref, ko, vo, kx, vx, do_ref, lse, dt, dq, dkv, dkvx):
    step = pl.program_id(0)
    rows = q_ref.shape[0]
    half = rows // 2
    first, tri = pair_masks(half, 1)
    highs = [meta[UPS + t] > 0 for t in range(others)]
    scale = (D // HEADS) ** -0.5

    def stats(part):
        both = [
            (lse[part, pl.ds(2 * step + h, 1), :], dt[part, pl.ds(2 * step + h, 1), :])
            for h in range(2)
        ]
        return tuple(jnp.concatenate(x, 1) for x in zip(*both))

    q_lo, q_hi = by_head(q_ref[:half], first), by_head(q_ref[half:], first)
    do_lo, do_hi = by_head(do_ref[:half], first), by_head(do_ref[half:], first)
    low = (q_lo, do_lo) + stats(0)
    high = (q_hi, do_hi) + stats(1)

    def tile(queries, k, v, diag):
        q, do, row_lse, row_dt = queries
        p = jnp.exp(dot_nt(k, q) - row_lse)
        if diag:
            p = jnp.where(tri, p, 0.0)
        ds = (p * (dot_nt(v, do) - row_dt)).astype(BF)
        return dot_tn(ds, k), dot(ds, q), dot(p.astype(BF), do)

    k_lo, k_hi, v_lo, v_hi = ko[0, :half], ko[0, half:], vo[0, :half], vo[0, half:]
    dq_lo, dk_a, dv_a = tile(low, k_lo, v_lo, True)
    dq_hi, dk_b, dv_b = tile(high, k_lo, v_lo, False)
    dkv[0, :half] = (dk_a + dk_b).astype(BF)
    dkv[1, :half] = (dv_a + dv_b).astype(BF)
    dq_add, dk, dv = tile(high, k_hi, v_hi, True)
    dq_hi = dq_hi + dq_add
    dkv[0, half:] = dk.astype(BF)
    dkv[1, half:] = dv.astype(BF)
    for t in range(others):
        up = highs[t]
        dq_add, dk, dv = tile(high, kx[t, 0, :half], vx[t, 0, :half], False)
        dq_hi = dq_hi + dq_add
        both = tuple(jnp.where(up, a, b) for a, b in zip(high, low))
        k_x = jnp.where(up, kx[t, 0, half:], kx[t, 0, :half])
        v_x = jnp.where(up, vx[t, 0, half:], vx[t, 0, :half])
        dq_add, dk_x, dv_x = tile(both, k_x, v_x, False)
        dq_hi = dq_hi + jnp.where(up, dq_add, 0.0)
        dq_lo = dq_lo + jnp.where(up, 0.0, dq_add)
        dkvx[t, 0, :half] = (dk + jnp.where(up, 0.0, dk_x)).astype(BF)
        dkvx[t, 1, :half] = (dv + jnp.where(up, 0.0, dv_x)).astype(BF)
        dkvx[t, 0, half:] = jnp.where(up, dk_x, 0.0).astype(BF)
        dkvx[t, 1, half:] = jnp.where(up, dv_x, 0.0).astype(BF)
    dq[:half] = (jnp.where(first, dq_lo[:half], dq_lo[half:]) * scale).astype(BF)
    dq[half:] = (jnp.where(first, dq_hi[:half], dq_hi[half:]) * scale).astype(BF)


def qkv_back_kernel(
    kinds, mode, others, meta, keep_ref, resid, dq, dkv, dkvx, d_middle, small_in, *rest
):
    nw = Weights.count(kinds)
    weights = Weights(kinds, rest[:nw], meta)
    rest = rest[nw:]
    done = mode > 0
    if done:
        prev_ref = rest[0]
        rest = rest[1:]
    nout = 2 if mode == 1 else 1
    dres = rest[0]
    rest = rest[1:]
    if done:
        done_mine, done_other = rest[:2]
        rest = rest[2:]
    if mode < 2:
        open_a = rest[0]
        rest = rest[1:]
    wqk, wv, prm, sems, osems = rest[:5]
    bufs = rest[5:]
    core = meta[CORE]
    keep = (keep_ref[0], keep_ref[1])
    weights.start_small(prm, sems.at[0])
    weights.start_qk(wqk, sems.at[1])
    weights.start_v(wv, sems.at[2])
    if done:
        prev_copy = pltpu.make_async_copy(prev_ref, bufs[-1], sems.at[3])
        prev_copy.start()
    landed(prm, sems.at[0])
    par = params_of(prm)
    xhat, rstd = norm_parts(resid[...])
    normed = jnp.transpose((xhat * par[0:1] + par[2:3]).astype(BF))
    parts = [dq[...]]
    for i in range(2):
        total = dkv[i].astype(F32)
        for t in range(others):
            total = total + dkvx[t, i].astype(F32)
        parts.append(total.astype(BF))
    landed(wqk, sems.at[1])
    landed(wv, sems.at[2])
    if done:
        prev_copy.wait()
    ws = [wqk[:, :, :GR, :], wqk[:, :, GR:, :], wv[...]]
    dy = 0.0
    for i, part in enumerate(parts):
        rows = slice(i * GR, (i + 1) * GR)
        dy = dy + dot_nt(part, ws[i].reshape(D, D))
        prev = bufs[-1][:, :, rows, :].reshape(D, D) if mode else None
        for which, val in enumerate(sort_terms(mode, keep, dot(normed, part), prev)):
            bufs[which][:, :, rows, :] = val.astype(BF).reshape(NG // 2, 2, GR, D)
    small = jnp.concatenate(
        [
            jnp.sum(dy * xhat, 0, keepdims=True),
            small_in[1:2],
            jnp.sum(dy, 0, keepdims=True),
            small_in[3:4],
            jnp.sum(parts[0].astype(F32), 0, keepdims=True),
            jnp.sum(parts[2].astype(F32), 0, keepdims=True),
            small_in[6:],
        ],
        0,
    )
    prev = bufs[-1][0, 0, 3 * GR :, :] if mode else None
    for which, val in enumerate(sort_terms(mode, keep, small, prev)):
        bufs[which][:, :, 3 * GR :, :] = jnp.broadcast_to(
            val.astype(BF)[None, None], (NG // 2, 2, SMALL, D)
        )
    later = []
    if done:
        later += to_cores(bufs[0], done_mine, done_other, core, osems.at[0], osems.at[1])
    if mode < 2:
        later.append(pltpu.make_async_copy(bufs[-1], open_a, osems.at[2]))
    for copy in later:
        copy.start()
    dres[...] = d_middle[...] + norm_back(xhat, rstd, par[0:1], dy)
    for copy in later:
        copy.wait()


def pack_kernel(meta, small_in, qkv, out, fc, proj, *rest):
    outs, smalls, sems = rest[:4], rest[4], rest[5]
    first, plane, at = meta[0], meta[1], meta[2]
    copies = []

    def cols(ref, src, i):
        return ref.at[src, :, pl.ds(i * D, D)]

    def copy(src, dst):
        copies.append(pltpu.make_async_copy(src, dst, sems.at[len(copies)]))
        copies[-1].start()

    for i, src in enumerate((first, 1 - first)):
        attn, ffn = outs[2 * i : 2 * i + 2]
        for k in range(NC // 2):
            col = pl.multiple_of((plane * (NC // 2) + k) * D, D)
            copy(fc.at[src, :, pl.ds(col, D)], ffn.at[pl.ds(k * GR, GR)])
        row = pl.multiple_of(plane * (PR // 2), 16)
        copy(proj.at[src, pl.ds(row, PR // 2)], ffn.at[pl.ds(NC // 2 * GR, PR // 2)])
        for k in range(3):
            copy(cols(qkv, src, k), attn.at[pl.ds(k * GR, GR)])
        copy(out.at[src], attn.at[pl.ds(3 * GR, GR)])

    lane = lax.broadcasted_iota(jnp.int32, (GR, D), 1)
    row = lax.broadcasted_iota(jnp.int32, (GR, D), 0)
    spread = jnp.where(lane == row + at * GR, 1.0, 0.0).astype(BF)
    lane = lax.broadcasted_iota(jnp.int32, (PR, D), 1)
    row = lax.broadcasted_iota(jnp.int32, (PR, D), 0)
    spread_h = jnp.where(lane == row + lax.rem(at, NG // NC) * PR, 1.0, 0.0).astype(BF)
    line = lax.broadcasted_iota(jnp.int32, (8, D), 0)
    for i, src in enumerate((first, 1 - first)):
        smalls[i, 0:8, :] = dot(small_in[src, :, :GR], spread).astype(BF)
        hid = dot(small_in[src, :, GR : GR + PR], spread_h)
        smalls[i, 8:16, :] = jnp.where(line == at // (NG // NC), hid[0:1], 0.0).astype(BF)
        copy(smalls.at[i], outs[2 * i].at[pl.ds(4 * GR, SMALL)])
    for one in copies:
        one.wait()


def assemble_kernel(meta, mine, other, whole, sems):
    copies = []
    for side, ref in enumerate((mine, other)):
        for low in range(2):
            for high in range(2):
                z = jnp.bitwise_xor(meta[ZPOS], low + 2 * high)
                y = meta[YPOS] if side == 0 else 1 - meta[YPOS]
                copies.append(
                    pltpu.make_async_copy(
                        ref.at[low, high], whole.at[z * 2 + y], sems.at[len(copies)]
                    )
                )
                copies[-1].start()
    for copy in copies:
        copy.wait()


def add_cores_kernel(segments, meta, mine, got, *outs):
    total = (mine[...].astype(F32) + got[...].astype(F32)).astype(BF)
    for i, (order, low, high, size) in enumerate(segments):
        if order == "x":
            sides, which = (total[:, low : low + size], total[:, high : high + size]), PLANE
        else:
            sides, which = (total[0:1, low : low + size], total[1:2, low : low + size]), YPOS
        outs[2 * i][...] = jnp.where(meta[which] == 0, sides[0], sides[1])
        outs[2 * i + 1][...] = jnp.where(meta[which] == 0, sides[1], sides[0])


def add_split_kernel(bits, meta, *refs):
    ins, outs = refs[: 2 * len(bits)], list(refs[2 * len(bits) :])
    for i, bit in enumerate(bits):
        mine, got = ins[2 * i], ins[2 * i + 1]
        if bit is None:
            outs.pop(0)[...] = (mine[0].astype(F32) + got[0].astype(F32)).astype(BF)
            continue
        keep, send = outs.pop(0), outs.pop(0)

        def pair(g, carry):
            for out, at in ((keep, 2 * g + meta[bit]), (send, 2 * g + 1 - meta[bit])):
                out[g] = (mine[at].astype(F32) + got[at].astype(F32)).astype(BF)
            return carry

        lax.fori_loop(0, mine.shape[0] // 2, pair, 0)


def finish_kernel(meta, *refs):
    ins, outs = refs[:12], refs[12:]
    qkv_g, out_g, fc_g, proj_g, gains_g, shifts_g, bias_g, hidden_g = outs
    first, plane, at = meta[0], meta[1], meta[2]
    low = lambda mine, peer: jnp.where(plane == 0, mine[...], peer[...])
    high = lambda mine, peer: jnp.where(plane == 0, peer[...], mine[...])
    pick = lax.broadcasted_iota(jnp.int32, (D, GR), 0) == (
        lax.broadcasted_iota(jnp.int32, (D, GR), 1) + at * GR
    )
    pick = jnp.where(pick, 1.0, 0.0).astype(BF)
    pick_h = lax.broadcasted_iota(jnp.int32, (D, PR), 0) == (
        lax.broadcasted_iota(jnp.int32, (D, PR), 1) + lax.rem(at, NG // NC) * PR
    )
    pick_h = jnp.where(pick_h, 1.0, 0.0).astype(BF)
    line = lax.broadcasted_iota(jnp.int32, (SMALL, D), 0)
    here = line == 8 + at // (NG // NC)

    for k, src in enumerate((1 - first, first)):
        pairs = ins[4 * k : 4 * k + 4] + ins[8 + 2 * k : 10 + 2 * k]
        halves = (low(*pairs[0:2]), high(*pairs[0:2]))
        for c in range(NC):
            half, at_row = divmod(c, NC // 2)
            rows = halves[half][at_row * GR : (at_row + 1) * GR]
            fc_g[src, :, c * D : (c + 1) * D] = rows.astype(F32)
        sums = pairs[2][...].astype(F32) + pairs[3][...].astype(F32)
        proj_g[src] = sums[:PR]
        out_g[src] = sums[PR:]
        attn = jnp.concatenate([low(*pairs[4:6]), high(*pairs[4:6])], 0)
        for c in range(3):
            qkv_g[src, :, c * D : (c + 1) * D] = attn[c * GR : (c + 1) * GR].astype(F32)
        small = attn[3 * GR :]
        vals = dot(small, pick)
        row = jnp.sum(jnp.where(here, small.astype(F32), 0.0), 0, keepdims=True)
        hid = dot(jnp.broadcast_to(row, (8, D)).astype(BF), pick_h)
        gains_g[src] = vals[0:2]
        shifts_g[src] = vals[2:4]
        bias_g[src] = vals[4:8]
        hidden_g[src] = hid[0:1]


VM = pl.BlockSpec(memory_space=pltpu.VMEM)
SM = pl.BlockSpec(memory_space=pltpu.SMEM)
HB = pl.BlockSpec(memory_space=pl.ANY)
DMA = pltpu.SemaphoreType.DMA


def call(kernel, outs, in_specs, out_specs, scratch, flops, name, weight=8, **more):
    cost = pl.CostEstimate(flops=int(flops * weight), bytes_accessed=1024, transcendentals=0)
    return pl.pallas_call(
        kernel,
        out_shape=outs,
        in_specs=in_specs,
        out_specs=out_specs,
        scratch_shapes=scratch,
        compiler_params=pltpu.CompilerParams(vmem_limit_bytes=VMEM_LIMIT),
        cost_estimate=cost,
        name=name,
        **more,
    )


def sds(shape, dtype):
    return jax.ShapeDtypeStruct(shape, dtype)


def run_qkv(meta, resid, kinds, weights):
    rows = resid.shape[0]
    return call(
        functools.partial(qkv_kernel, kinds),
        (sds((rows, D), BF), sds((2, rows, D), BF)),
        [SM, VM] + [HB] * len(weights),
        (VM, VM),
        qkv_scratch() + [DMA((3,))],
        2 * rows * D * 3 * D,
        "qkv",
        8 if len(kinds) > 1 else 0.01,
    )(meta, resid, *weights)


def qkv_scratch():
    return [
        pltpu.VMEM((NG // 2, 2, 2 * GR, D), BF),
        pltpu.VMEM((NG // 2, 2, GR, D), BF),
        pltpu.VMEM((NG // 2, 2, SMALL, D), BF),
    ]


def pair_specs(rows, others):
    lanes = 2 * D // HEADS
    return [
        SM,
        pl.BlockSpec((rows, lanes), lambda i: (0, i)),
        pl.BlockSpec((1, rows, lanes), lambda i: (0, 0, i)),
        pl.BlockSpec((1, rows, lanes), lambda i: (1, 0, i)),
        pl.BlockSpec((others, 1, rows, lanes), lambda i: (0, 0, 0, i)),
        pl.BlockSpec((others, 1, rows, lanes), lambda i: (0, 1, 0, i)),
    ]


def run_attn(meta, q, kv, kvx, weight):
    rows, others = q.shape[0], kvx.shape[0]
    half = rows // 2
    return call(
        functools.partial(attn_fwd_kernel, others),
        (sds((rows, D), BF), sds((2, 16, half), F32)),
        pair_specs(rows, others),
        (
            pl.BlockSpec((rows, 2 * D // HEADS), lambda i: (0, i)),
            pl.BlockSpec((2, 16, half), lambda i: (0, 0, 0)),
        ),
        [pltpu.VMEM((rows, 128), F32)],
        HEADS * (3 + 2 * others) * half * half * 256 * 4,
        "attn",
        weight,
        grid=(PAIRS,),
    )(meta, q, kv, kv, kvx, kvx)


def weight_scratch(rows, flipped=False):
    shape = (D, rows) if flipped else (rows, D)
    return [
        pltpu.VMEM((NG // 2, 2, GR, D), BF),
        pltpu.VMEM((NG // 2, 2, SMALL, D), BF),
        pltpu.VMEM((NC, NG // 2, 2, GR, D), BF),
        pltpu.VMEM((NC, NG // 2 // NC, 2, PR, D), BF),
        pltpu.VMEM(shape, BF),
        pltpu.VMEM(shape, F32),
        pltpu.VMEM((SMALL, D), F32),
    ]


def run_mlp(meta, resid, mixed, kinds, weights):
    rows = resid.shape[0]
    return call(
        functools.partial(mlp_kernel, kinds),
        (sds((rows, D), F32), sds((NC, rows, D), BF), sds((rows, D), F32)),
        [SM, VM, VM] + [HB] * len(weights),
        (VM, VM, VM),
        weight_scratch(rows) + [DMA((2 + 2 * NC,))],
        2 * rows * D * (D + 2 * FF),
        "mlp",
        8 if len(kinds) > 1 else 0.01,
    )(meta, resid, mixed, *weights)


def run_mlp_back(mode, meta, keep, dres, mid, pre, mixed, kinds, weights, prev):
    rows = dres.shape[0]
    nout = 2 if mode == 1 else 1
    b_rows = NC * GR + PR
    o_shape = sds((NG // 2, 2, GR, D), BF)
    outs = ()
    if mode:
        outs += (sds((NG // 2, b_rows + GR, D), BF),) * 2
    if mode < 2:
        outs += (sds((NG // 2, 2, b_rows, D), BF), o_shape)
    stage = [
        pltpu.VMEM((2, NG // 2, 2, GR, D), BF),
        pltpu.VMEM((2, NG // 2 // NC, 2, PR, D), BF),
        pltpu.VMEM((NG // 2, 2, GR, D), BF),
    ] * nout
    return call(
        functools.partial(mlp_back_kernel, kinds, mode),
        (
            sds((rows, D), F32),
            sds((rows, D), BF),
            sds((2, 16, rows // 2), F32),
            sds((SMALL, D), F32),
        )
        + outs,
        [SM, SM, VM, VM, VM, VM] + [HB] * (len(weights) + len(prev)),
        (VM, VM, VM, VM) + (HB,) * len(outs),
        weight_scratch(rows, True)
        + [pltpu.VMEM((rows, D), BF), DMA((3 + 4 * NC,)), DMA((8, NC))]
        + stage,
        4 * rows * D * (D + 2 * FF),
        "mlp_back",
    )(meta, keep, dres, mid, pre, mixed, *weights, *prev)


def run_attn_back(meta, q, kv, kvx, d_mixed, lse, dt):
    rows, others = q.shape[0], kvx.shape[0]
    half = rows // 2
    lanes = 2 * D // HEADS
    stat = pl.BlockSpec((2, 16, half), lambda i: (0, 0, 0))
    block = pl.BlockSpec((rows, lanes), lambda i: (0, i))
    return call(
        functools.partial(attn_back_kernel, others),
        (sds((rows, D), BF), sds((2, rows, D), BF), sds((others, 2, rows, D), BF)),
        pair_specs(rows, others) + [block, stat, stat],
        (
            block,
            pl.BlockSpec((2, rows, lanes), lambda i: (0, 0, i)),
            pl.BlockSpec((others, 2, rows, lanes), lambda i: (0, 0, 0, i)),
        ),
        [],
        HEADS * (3 + 2 * others) * half * half * 256 * 10,
        "attn_back",
        grid=(PAIRS,),
    )(meta, q, kv, kv, kvx, kvx, d_mixed, lse, dt)


def run_qkv_back(
    mode, meta, keep, resid, dq, dkv, dkvx, d_middle, small, kinds, weights, prev
):
    rows, others = resid.shape[0], dkvx.shape[0]
    nout = 2 if mode == 1 else 1
    shape = (NG // 2, 2, 3 * GR + SMALL, D)
    outs = ()
    if mode:
        outs += (sds((NG // 2, 3 * GR + SMALL, D), BF),) * 2
    if mode < 2:
        outs += (sds(shape, BF),)
    return call(
        functools.partial(qkv_back_kernel, kinds, mode, others),
        (sds((rows, D), F32),) + outs,
        [SM, SM] + [VM] * 6 + [HB] * (len(weights) + len(prev)),
        (VM,) + (HB,) * len(outs),
        qkv_scratch() + [DMA((4,)), DMA((3,))] + [pltpu.VMEM(shape, BF)] * nout,
        4 * rows * D * 3 * D,
        "qkv_back",
    )(meta, keep, resid, dq, dkv, dkvx, d_middle, small, *weights, *prev)


def run_pack(meta, small, qkv, out, fc, proj):
    rows = (A_ROWS, B_ROWS // 2) * 2
    return call(
        pack_kernel,
        tuple(sds((r, D), BF) for r in rows),
        [SM, VM] + [HB] * 4,
        (HB,) * 4,
        [pltpu.VMEM((2, SMALL, D), BF), DMA((2 * (NC // 2 + 6),))],
        2 * 16 * PR * D,
        "pack",
    )(meta, small, qkv, out, fc, proj)


def run_assemble(meta, mine, other):
    rows = mine.shape[-2]
    return call(
        assemble_kernel,
        sds((NG // 2, rows, D), BF),
        [SM, HB, HB],
        VM,
        [DMA((NG // 2,))],
        NG * rows * D,
        "assemble",
    )(meta, mine, other)


def run_add_cores(meta, mine, got, segments, weight):
    groups, rows = mine.shape[:2]
    outs, specs = [], []
    for order, _, _, size in segments:
        step = 2 if order == "x" else 1
        outs += [sds((groups // 2 * step, size, D), BF)] * 2
        specs += [pl.BlockSpec((step, size, D), lambda i: (i, 0, 0))] * 2
    block = pl.BlockSpec((2, rows, D), lambda i: (i, 0, 0))
    return call(
        functools.partial(add_cores_kernel, segments),
        outs,
        [SM, block, block],
        specs,
        [],
        mine.size * weight,
        "add_cores",
        grid=(groups // 2,),
    )(meta, mine, got)


def run_add_split(meta, bits, pairs, weight):
    outs = []
    for bit, (mine, _) in zip(bits, pairs):
        groups, rows = mine.shape[:2]
        if bit is None:
            outs.append(sds((rows, D), BF))
        else:
            outs += [sds((groups // 2, rows, D), BF)] * 2
    ins = [x for pair in pairs for x in pair]
    return call(
        functools.partial(add_split_kernel, bits),
        outs,
        [SM] + [VM] * len(ins),
        [VM] * len(outs),
        [],
        sum(x.size for x in ins) * weight,
        "add_split",
    )(meta, *ins)


def run_finish(meta, parts):
    outs = (
        sds((2, GR, 3 * D), F32),
        sds((2, GR, D), F32),
        sds((2, GR, FF), F32),
        sds((2, PR, D), F32),
        sds((2, 2, GR), F32),
        sds((2, 2, GR), F32),
        sds((2, 4, GR), F32),
        sds((2, 1, PR), F32),
    )
    return call(
        finish_kernel, outs, [SM] + [VM] * len(parts), (VM,) * 8, [], 2**20, "finish"
    )(meta, *parts)


def regroup(packed, own_from, own_to, widths):
    if own_from == own_to:
        return packed
    parts, at = [], 0
    for width in widths:
        rows = width // own_from
        part = packed[:, at : at + rows].reshape(width, D)
        parts.append(part.reshape(own_to, width // own_to, D))
        at += rows
    return jnp.concatenate(parts, 1)


def blocks(table):
    return jnp.concatenate([table[:, i : i + D] for i in range(0, table.shape[1], D)], 0)


def unblock(rows, count):
    size = rows.shape[0] // count
    return jnp.concatenate([rows[i * size : (i + 1) * size] for i in range(count)], 1)


def place_small(gains, shifts, bias_m, bias_h, at):
    vecs = jnp.concatenate([gains, shifts, bias_m], 0)
    wide = lax.dynamic_update_slice(jnp.zeros((8, D), BF), vecs, (0, at * vecs.shape[1]))
    hid = lax.dynamic_update_slice(jnp.zeros((FF,), BF), bias_h, (at * bias_h.shape[0],))
    return jnp.concatenate([wide, hid.reshape(NC, D), jnp.zeros((SMALL - 8 - NC, D), BF)], 0)


def per_device(own, n, tokens, tie, qkv_w, out_w, fc_w, proj_w, gains, shifts, bias_m, bias_h, cotangent):
    axes = ("own", "dp")
    o = lax.axis_index("own")
    d = lax.axis_index("dp")
    core = o % 2
    rows = tokens.shape[1]
    half = rows // 2
    others = n - 1

    def at(pair, s, j):
        return (2 * pair + j % 2) * n + s * (n // 2) + j // 2

    j = (d % (n // 2)) * 2 + core

    def place(block):
        return block if block < n else 2 * n - 1 - block

    def moves(odd):
        return [
            ((2 * pair + s) * n + dd, at(pair, s, place(2 * dd + odd)))
            for pair in range(own // 2)
            for s in range(2)
            for dd in range(n)
        ]

    def to_chip(x):
        x = x.reshape(rows, D)
        even = lax.ppermute(x[:half], axes, moves(0))
        odd = lax.ppermute(x[half:], axes, moves(1))
        return jnp.concatenate(
            [jnp.where(core == 0, even, odd), jnp.where(core == 0, odd, even)], 0
        )

    def from_chip(x):
        back = [[(b, a) for a, b in moves(odd)] for odd in range(2)]
        even = lax.ppermute(jnp.where(core == 0, x[:half], x[half:]), axes, back[0])
        odd = lax.ppermute(jnp.where(core == 0, x[half:], x[:half]), axes, back[1])
        return jnp.concatenate([even, odd], 0).reshape(tokens.shape)

    def shift(x, step):
        pairs = [
            (at(pair, s, (place_ + step) % n), at(pair, s, place_))
            for pair in range(own // 2)
            for s in range(2)
            for place_ in range(n)
        ]
        return lax.ppermute(x, axes, pairs)

    plane, y, z = d % 2, (o // 2) % 2, o // 4
    nz = own // 4

    def device(zz, yy, cc, dd):
        return ((zz * 2 + yy) * 2 + cc) * n + dd

    everyone = [
        (zz, yy, cc, dd)
        for zz in range(nz)
        for yy in range(2)
        for cc in range(2)
        for dd in range(n)
    ]

    def swap(x, axis):
        turn = {
            "core": lambda zz, yy, cc, dd: device(zz, yy, 1 - cc, dd),
            "y": lambda zz, yy, cc, dd: device(zz, 1 - yy, cc, dd),
            "x": lambda zz, yy, cc, dd: device(zz, yy, cc, dd ^ 1),
            "z1": lambda zz, yy, cc, dd: device(zz ^ 1, yy, cc, dd),
            "z2": lambda zz, yy, cc, dd: device(zz ^ 2, yy, cc, dd),
        }[axis]
        return lax.ppermute(x, axes, [(device(*at_), turn(*at_)) for at_ in everyone])

    def from_z(x, step):
        pairs = [
            (device((zz + step) % nz, yy, cc, dd), device(zz, yy, cc, dd))
            for zz, yy, cc, dd in everyone
        ]
        return lax.ppermute(x, axes, pairs)

    def after(x, *deps):
        return lax.optimization_barrier((x, *deps))[0]

    def after_all(xs, *deps):
        return lax.optimization_barrier((tuple(xs), *deps))[0]

    open_src = tie[0]
    isin = lambda u: (tie[u] != open_src).astype(jnp.int32)
    ups = [((j + t) % n > j).astype(jnp.int32) for t in range(1, n)]
    metas = [jnp.stack([isin(u), core, plane, y, z, z % 2, z // 2] + ups).astype(jnp.int32) for u in range(3)]
    keep = jnp.stack([isin(1), isin(2)]).astype(F32)
    direct = own == NG and n == 2

    if direct:
        small = jnp.concatenate([gains, shifts, bias_m], 1)
        hid = jnp.broadcast_to(bias_h[:, None], (2, 8, bias_h.shape[1]))
        packed = run_pack(
            jnp.stack([open_src, plane, o]).astype(jnp.int32),
            jnp.concatenate([small, hid], 2),
            qkv_w,
            out_w,
            fc_w,
            proj_w,
        )

        def square(x, axis):
            return jnp.stack([x, swap(x, axis)], 0)

        def cores_of(part):
            return [part, swap(part, "core")]

        twos, lines, sides = [], [], []
        for part in (packed[1], packed[3], packed[0], packed[2]):
            twos.append(square(after(part, twos[-1]) if twos else part, "z2"))
            two = after(twos[-1], lines[-1]) if lines else twos[-1]
            lines.append(square(two, "z1"))
            line = after(lines[-1], sides[-1][1]) if sides else lines[-1]
            sides.append((line, swap(line, "y")))
        resid = to_chip(after(tokens, twos[0])).astype(F32)
        dres = to_chip(after(cotangent, twos[0])).astype(F32)
        ffn = [run_assemble(after(metas[0], resid, dres, lines[1]), *sides[0])]
        peers = [swap(ffn[0], "x")]
        ffn.append(run_assemble(after(metas[0], lines[2]), *sides[1]))
        peers.append(swap(after(ffn[1], peers[0]), "x"))
        attn = run_assemble(after(metas[0], lines[3]), *sides[2])
        first_a, first_b = cores_of(attn), cores_of(ffn[0]) + cores_of(peers[0])
        kinds = (("a2", "b4"),) * 2
        second_b = cores_of(ffn[1]) + cores_of(peers[1])
        metas[0] = after(metas[0], *first_a, *first_b, *second_b[:2])
    else:
        resid = to_chip(tokens).astype(F32)
        dres = to_chip(cotangent).astype(F32)
        sources = []
        for src in (open_src, 1 - open_src):
            pick = lambda table: lax.dynamic_index_in_dim(table, src, 0, keepdims=False)
            part = jnp.concatenate(
                [blocks(pick(qkv_w)), pick(out_w), blocks(pick(fc_w)), pick(proj_w)], 0
            )
            full = lax.all_gather(part, "own", axis=0, tiled=False)
            full = regroup(full, own, NG, [D] * (4 + NC) + [FF])
            small = place_small(pick(gains), pick(shifts), pick(bias_m), pick(bias_h), o)
            small = lax.psum(small.astype(F32), "own").astype(BF)
            small = jnp.concatenate([small[None], jnp.zeros((NG - 1, SMALL, D), BF)], 0)
            full = jnp.concatenate([full[:, : 4 * GR], small, full[:, 4 * GR :]], 1)
            sources.append([full.reshape(NG // 2, 2, -1, D)])
        first_a = first_b = sources[0]
        second_a = second_b = sources[1]
        kinds = (("a", "b"),) * 2

    def weights_of(u, attn_only=False):
        many = 1 if u == 0 else 2
        arrays = first_a + ([] if attn_only else first_b)
        if u:
            arrays = arrays + second_a + ([] if attn_only else second_b)
        return tuple(kind[: 1 if attn_only else 2] for kind in kinds[:many]), arrays

    saved = []
    for u in range(3):
        meta = metas[u]
        q, kv = run_qkv(meta, resid, *weights_of(u, True))
        kvx = jnp.stack([shift(kv, t) for t in range(1, n)], 0)
        mixed, lse = run_attn(meta, q, kv, kvx, 8 if u else 0.01)
        middle, pre, result = run_mlp(meta, resid, mixed, *weights_of(u))
        if u == 0 and direct:
            second_a = cores_of(run_assemble(after(metas[1], middle, peers[1]), *sides[3]))
            metas[1] = after(metas[1], *second_a)
        saved.append((resid, q, kv, kvx, mixed, lse, middle, pre))
        resid = result
    output = from_chip(resid.astype(BF))

    def scatter_full(mine, other, widths, small_rows):
        pair = jnp.where(core == 0, jnp.stack([mine, other], 1), jnp.stack([other, mine], 1))
        grad = pair.reshape(NG, -1, D)
        body = grad.shape[1] - small_rows
        tail = grad[:1, body:]
        grad = regroup(grad[:, :body], NG, own, widths)
        if small_rows:
            tail = jnp.broadcast_to(tail, (own, small_rows, D))
            grad = jnp.concatenate([grad, tail], 1)
        part = lax.psum_scatter(grad, "own", scatter_dimension=0, tiled=False)
        return lax.psum(part, "dp").astype(F32)


    class Scatter:
        NEXT = {"x": ("y", YPOS), "y": ("z1", ZLOW), "z1": ("z2", ZHIGH), "z2": ("x", None)}

        def __init__(self, order, keep_, send):
            self.stage, self.keep, self.done = order, keep_, None
            self.got = swap(send, order)

    def step(meta, chunks, weight=1):
        moves_ = [Scatter.NEXT[one.stage] for one in chunks]
        outs = run_add_split(
            meta,
            tuple(bit for _, bit in moves_),
            [(one.keep, one.got) for one in chunks],
            weight,
        )
        first_out, outs = outs[0], list(outs)
        for one, (stage, bit) in zip(chunks, moves_):
            one.stage = stage
            one.keep = outs.pop(0)
            one.got = swap(one.keep if bit is None else outs.pop(0), stage)
            if bit is None:
                one.done = [one.keep, one.got]
        return first_out

    def scatter_start(meta, mine, got, segs, weight):
        outs = run_add_cores(meta, mine, got, segs, weight)
        return [Scatter(seg[0], *outs[2 * i : 2 * i + 2]) for i, seg in enumerate(segs)], outs[0]

    in_rows, a_rows = NC // 2 * GR, 4 * GR + SMALL
    b_segs = (("x", 0, in_rows, in_rows), ("y", NC * GR, 0, PR + GR))
    half_a = (3 * GR + SMALL) // 2
    a_segs = (("x", 0, half_a, half_a),)

    prev_b, prev_a = [], []
    shares, fin, opn = {}, [], []
    wr, pr = D // own, FF // own
    for u in (2, 1, 0):
        mode = 2 - u
        meta = metas[u]
        resid, q, kv, kvx, mixed, lse, middle, pre = saved[u]
        outs = run_mlp_back(
            mode, meta, keep, dres, middle, pre, mixed, *weights_of(u), prev_b
        )
        d_middle, d_mixed, dt, small = outs[:4]
        if mode:
            mine_b, other_b = outs[4:6]
            if direct:
                got_b = swap(other_b, "core")
        prev_b = list(outs[-2:])
        if mode == 0:
            meta = after(meta, output)
        if mode == 2 and direct:
            slot = after(meta, d_mixed)
            more, last = scatter_start(slot, *fin_a, a_segs, 1)
            last = step(after(slot, last), fin, 4096)
            fin += more
            opn, last = scatter_start(after(slot, last), mine_b, got_b, b_segs, 1)
            meta = after(meta, last)
        dq, dkv, dkvx = run_attn_back(meta, q, kv, kvx, d_mixed, lse, dt)
        back = jnp.stack([shift(dkvx[t - 1], n - t) for t in range(1, n)], 0)
        if mode and direct:
            slot = after(meta, dq)
            if mode == 1:
                fin, last = scatter_start(slot, mine_b, got_b, b_segs, 4096)
            else:
                last = step(slot, fin, 4096)
            meta = after(meta, last)
        outs = run_qkv_back(
            mode,
            meta,
            keep,
            resid,
            dq,
            dkv,
            back,
            d_middle,
            small,
            *weights_of(u, True),
            prev_a,
        )
        dres = outs[0]
        prev_a = [outs[-1]]
        if not mode:
            continue
        mine_a, other_a = outs[1:3]
        if direct:
            if mode == 1:
                fin_a = (mine_a, swap(other_a, "core"))
            else:
                slot = after(metas[0], dres)
                got_a = swap(other_a, "core")
                last = step(slot, fin, 4096)
                more, last = scatter_start(after(slot, last), mine_a, got_a, a_segs, 1)
                left = [one for one in fin if one.done is None]
                last = step(after(slot, last), left)
                last = step(after(slot, last), opn, 1)
                chunks = fin[:2] + opn + fin[2:] + more
                old = []
                while any(one.done is None for one in chunks):
                    for group, weight in ((more, 16384), (fin + opn, 1)):
                        left = [one for one in group if one.done is None]
                        if left:
                            last = step(after(slot, last, *old), left, weight)
                            old = [one.got for one in left if one.done]
                done = [x for one in chunks for x in one.done]
        else:
            g_b = scatter_full(mine_b, other_b, [D] * NC + [FF, D], 0)
            g_in, g_proj, g_out = jnp.split(g_b, [NC * wr, NC * wr + pr])
            g_a = scatter_full(mine_a, other_a, [D] * 3, SMALL)
            g_a = jnp.concatenate([g_a[: 3 * wr], g_out, g_a[3 * wr :]], 0)
            shares[mode] = (g_a, g_in, g_proj)
    input_grad = from_chip(dres.astype(BF))

    if direct:
        place_meta = jnp.stack([open_src, plane, o]).astype(jnp.int32)
        grads = list(run_finish(place_meta, done))
        grads[-1] = grads[-1].reshape(2, -1)
        return (output, input_grad, *grads)

    flip = open_src == 0

    def both(make):
        fin, opn = make(*shares[1]), make(*shares[2])
        return jnp.stack([jnp.where(flip, opn, fin), jnp.where(flip, fin, opn)], 0)

    def lanes(a, lo, hi):
        at_row = 4 * wr
        return lax.dynamic_slice(a[at_row + lo : at_row + hi], (0, o * wr), (hi - lo, wr))

    def hidden(a):
        return lax.dynamic_slice(a[4 * wr + 8 : 4 * wr + 8 + NC].reshape(FF), (o * pr,), (pr,))

    return (
        output,
        input_grad,
        both(lambda a, f, p: unblock(a[: 3 * wr], 3)),
        both(lambda a, f, p: a[3 * wr : 4 * wr]),
        both(lambda a, f, p: unblock(f, NC)),
        both(lambda a, f, p: p),
        both(lambda a, f, p: lanes(a, 0, 2)),
        both(lambda a, f, p: lanes(a, 2, 4)),
        both(lambda a, f, p: lanes(a, 4, 8)),
        both(lambda a, f, p: hidden(a)),
    )


def solution(mesh):
    return jax.shard_map(
        functools.partial(per_device, mesh.shape["own"], mesh.shape["dp"]),
        mesh=mesh,
        in_specs=(
            P("own", "dp", None),
            P(),
            P(None, "own", None),
            P(None, "own", None),
            P(None, "own", None),
            P(None, "own", None),
            P(None, None, "own"),
            P(None, None, "own"),
            P(None, None, "own"),
            P(None, "own"),
            P("own", "dp", None),
        ),
        out_specs=(
            P("own", "dp", None),
            P("own", "dp", None),
            P(None, "own", None),
            P(None, "own", None),
            P(None, "own", None),
            P(None, "own", None),
            P(None, None, "own"),
            P(None, None, "own"),
            P(None, None, "own"),
            P(None, "own"),
        ),
        check_vma=False,
    )
```
